32 devices in a mesh: fsdp: 16 (over z, y, x), rep: 2 (over core).
Axes of the slice: x: 2, y: 2, z: 4, core: 2. Of those that a mesh axis runs over, the one named last changes fastest.
Arguments:
- tokens: bfloat16 [32, 128, 1152], P(('fsdp', 'rep')), may hold values from -6 to 6
- segment_ids: int32 [32, 128], P(('fsdp', 'rep')), may hold values from 0 to 2, never falling along the last dimension, each value on 1 to 64 neighbouring positions
- w_query: bfloat16 [1152, 1024], P('fsdp'), may hold values from -0.1875 to 0.1875
- w_key: bfloat16 [1152, 256], P('fsdp'), may hold values from -0.1875 to 0.1875
- w_value: bfloat16 [1152, 256], P('fsdp'), may hold values from -0.1875 to 0.1875
- w_out: bfloat16 [1024, 1152], P(None, 'fsdp'), may hold values from -0.1875 to 0.1875
- w_gate: bfloat16 [1152, 6912], P('fsdp'), may hold values from -0.1875 to 0.1875
- w_up: bfloat16 [1152, 6912], P('fsdp'), may hold values from -0.1875 to 0.1875
- w_down: bfloat16 [6912, 1152], P(None, 'fsdp'), may hold values from -0.078125 to 0.078125
- g_attn_in: bfloat16 [1152], P('fsdp'), may hold values from 0.25 to 1.75
- g_attn_out: bfloat16 [1152], P('fsdp'), may hold values from 0.25 to 1.75
- g_ffn_in: bfloat16 [1152], P('fsdp'), may hold values from 0.25 to 1.75
- g_ffn_out: bfloat16 [1152], P('fsdp'), may hold values from 0.25 to 1.75
- g_query: bfloat16 [256], replicated, may hold values from 0.25 to 1.75
- g_key: bfloat16 [256], replicated, may hold values from 0.25 to 1.75
- cotangent: bfloat16 [32, 128, 1152], P(('fsdp', 'rep')), may hold values from -6 to 6
Outputs:
- activations: bfloat16 [32, 128, 1152], P(('fsdp', 'rep'))
- input_grad: bfloat16 [32, 128, 1152], P(('fsdp', 'rep'))
- query_grad: float32 [1152, 1024], P('fsdp')
- key_grad: float32 [1152, 256], P('fsdp')
- value_grad: float32 [1152, 256], P('fsdp')
- out_grad: float32 [1024, 1152], P(None, 'fsdp')
- gate_grad: float32 [1152, 6912], P('fsdp')
- up_grad: float32 [1152, 6912], P('fsdp')
- down_grad: float32 [6912, 1152], P(None, 'fsdp')
- attn_in_grad: float32 [1152], P('fsdp')
- attn_out_grad: float32 [1152], P('fsdp')
- ffn_in_grad: float32 [1152], P('fsdp')
- ffn_out_grad: float32 [1152], P('fsdp')
- query_gain_grad: float32 [256], replicated
- key_gain_grad: float32 [256], replicated
The draws below stay inside these ranges and needn't reach their ends.
Inputs may be any that keep to these rules, and one draw needn't show every extreme that they name: `segment_ids`: along each row the ids never fall; each of the ids 0, 1 and 2 names 1 to 64 neighbouring tokens, and one of them names exactly 64.
All inputs are finite; a program needn't handle non-finite values.
Results may differ from the reference program's by a relative error of at most 0.015.
Values may be sent and summed in bfloat16 or wider, within the bound.
No kernel may reach another device: no remote copies, remote signals or barrier semaphores. Data moves between devices by JAX's collectives and lax.ppermute only.
A program may use at most 256 MiB of HBM per device.

```python
import math
import jax
import jax.numpy as jnp
import numpy as np
from jax import lax

D = 1152
HEADS = 4
HEAD_DIM = 256
FF = 6912
ROW = 128
ROWS = 32


def levels(own_key, dims, split, smallest, largest):
    loudness, own = 1.0, jax.random.fold_in(own_key, 6)
    for axis_at, shards_of in split:
        draws = jnp.exp(jax.random.uniform(jax.random.fold_in(own, axis_at), (shards_of,), jnp.float32, smallest / len(split), largest / len(split)))
        loudness = loudness * jnp.repeat(draws, dims[axis_at] // shards_of).reshape([-1 if axis == axis_at else 1 for axis in range(len(dims))])
    return loudness


def profile(number_of, total, most, lean):
    weights = [(1 << 20) // math.isqrt(grade ** lean) + 1 for grade in range(2, number_of + 1)]
    rest, holding = total - most - (number_of - 1), [1] * (number_of - 1)
    while rest > 0:
        candidates = [i for i in range(number_of - 1) if holding[i] < most]
        pool, remaining = sum([weights[i] for i in candidates]), rest
        for i in candidates:
            addition = min(most - holding[i], max(1, remaining * weights[i] // pool), rest)
            holding[i] = holding[i] + addition
            rest = rest - addition
    return np.array([most] + holding)


def uneven(stream_key, amount, total, bound, skew):
    if amount == 2:
        one = jax.random.randint(stream_key, (), max(1, total - bound), min(bound, total - 1) + 1)
        return jnp.stack([one, total - one])
    lengths = jnp.asarray(profile(amount, total, bound, skew), jnp.int32)
    pairs = (amount - 1) // 2
    donor, receiver = lengths[1:1 + 2 * pairs:2], lengths[2:2 + 2 * pairs:2]
    slack = jnp.minimum(donor - 1, bound - receiver)
    passed = jax.random.randint(jax.random.fold_in(stream_key, 1), (pairs,), 0, 1 << 20) % (slack + 1)
    lengths = lengths.at[1:1 + 2 * pairs:2].set(donor - passed).at[2:2 + 2 * pairs:2].set(receiver + passed)
    return lengths[jax.random.permutation(jax.random.fold_in(stream_key, 2), amount)]


def noise(rng, dims, spread, limit, pieces=(), kind=jnp.bfloat16):
    array = spread * jax.random.normal(rng, dims, jnp.float32)
    if pieces:
        array = array * levels(rng, dims, pieces, -0.22, 0.18)
    return jnp.clip(array, -limit, limit).astype(kind)


def setup_inputs(seed: int = 0) -> dict:
    splits = jax.random.split(jax.random.key(seed), 17)
    return {
        "tokens": noise(splits[0], (ROWS, ROW, D), 1.0, 6.0, ((0, 32),)),
        "segment_ids": jax.vmap(lambda own: jnp.searchsorted(jnp.cumsum(uneven(own, max(ROW // 64, 3), ROW, ROW // 2, 2)), jnp.arange(ROW), side="right"))(jax.random.split(splits[1], ROWS)).reshape((ROWS, ROW)).astype(jnp.int32),
        "w_query": noise(splits[2], (D, HEADS * HEAD_DIM), D ** -0.5, 0.1875, ((0, 16),)),
        "w_key": noise(splits[3], (D, HEAD_DIM), D ** -0.5, 0.1875, ((0, 16),)),
        "w_value": noise(splits[4], (D, HEAD_DIM), D ** -0.5, 0.1875, ((0, 16),)),
        "w_out": noise(splits[5], (HEADS * HEAD_DIM, D), (HEADS * HEAD_DIM) ** -0.5, 0.1875, ((1, 16),)),
        "w_gate": noise(splits[6], (D, FF), D ** -0.5, 0.1875, ((0, 16),)),
        "w_up": noise(splits[7], (D, FF), D ** -0.5, 0.1875, ((0, 16),)),
        "w_down": noise(splits[8], (FF, D), FF ** -0.5, 0.078125, ((1, 16),)),
        "g_attn_in": jnp.clip(1.0 + 0.15 * jax.random.normal(splits[9], (D,), jnp.float32), 0.25, 1.75).astype(jnp.bfloat16),
        "g_attn_out": jnp.clip(1.0 + 0.15 * jax.random.normal(splits[10], (D,), jnp.float32), 0.25, 1.75).astype(jnp.bfloat16),
        "g_ffn_in": jnp.clip(1.0 + 0.15 * jax.random.normal(splits[11], (D,), jnp.float32), 0.25, 1.75).astype(jnp.bfloat16),
        "g_ffn_out": jnp.clip(1.0 + 0.15 * jax.random.normal(splits[12], (D,), jnp.float32), 0.25, 1.75).astype(jnp.bfloat16),
        "g_query": jnp.clip(1.0 + 0.15 * jax.random.normal(splits[13], (HEAD_DIM,), jnp.float32), 0.25, 1.75).astype(jnp.bfloat16),
        "g_key": jnp.clip(1.0 + 0.15 * jax.random.normal(splits[14], (HEAD_DIM,), jnp.float32), 0.25, 1.75).astype(jnp.bfloat16),
        "cotangent": noise(splits[15], (ROWS, ROW, D), 1.0, 6.0, ((0, 32),)),
    }


@jax.custom_vjp
def low(v):
    return lax.optimization_barrier(v.astype(jnp.bfloat16)).astype(jnp.float32)

@jax.custom_vjp
def low_back(v):
    return v

def low_keep(v):
    return (low(v), None)

def low_pass(kept, grad):
    return (grad,)

def back_keep(v):
    return (v, None)

def back_low(kept, grad):
    return (low(grad),)
low.defvjp(low_keep, low_pass)
low_back.defvjp(back_keep, back_low)
eps = 1e-06

def rms_norm(value, gain):
    return value * lax.rsqrt(lax.optimization_barrier(jnp.mean(value * value, axis=-1, keepdims=True)) + eps) * gain

def matmul(left, right):
    return jnp.dot(left, right, precision=lax.Precision.HIGHEST)

def positions(segments):
    earlier = (segments[None, :] < segments[:, None]).astype(jnp.int32)
    return jnp.arange(segments.shape[0], dtype=jnp.int32) - lax.optimization_barrier(jnp.sum(earlier, axis=1))

def rope_tables(where, width):
    half = width // 2
    expo = jnp.arange(half, dtype=jnp.float32) * (2.0 / width)
    freq = jnp.exp(-expo * jnp.log(1000000.0))
    angle = where.astype(jnp.float32)[:, None] * freq[None, :]
    return (jnp.cos(angle), jnp.sin(angle))

def rotate(value, cosine, sine):
    half = value.shape[-1] // 2
    first = value[..., :half]
    second = value[..., half:]
    cosine = cosine[:, None, :]
    sine = sine[:, None, :]
    return jnp.concatenate([first * cosine - second * sine, second * cosine + first * sine], axis=-1)

def layer_row(source, segments, weights):
    query_w, key_w, value_w, out_w, gate_w, up_w, down_w, attn_in_gain, attn_out_gain, ffn_in_gain, ffn_out_gain, query_gain, key_gain = weights
    length = source.shape[0]
    scale = HEAD_DIM ** (-0.5)
    normed = low(rms_norm(source, attn_in_gain))
    query = low_back(matmul(normed, query_w)).reshape(length, HEADS, HEAD_DIM)
    keys = low_back(matmul(normed, key_w)).reshape(length, 1, HEAD_DIM)
    values = low(low_back(matmul(normed, value_w)))
    cosine, sine = rope_tables(positions(segments), HEAD_DIM)
    query = low(low_back(rotate(rms_norm(query, query_gain), cosine, sine)))
    keys = low(low_back(rotate(rms_norm(keys, key_gain), cosine, sine)))[:, 0, :]
    raw = low_back(jnp.einsum('shd,td->hst', query, keys, precision=lax.Precision.HIGHEST))
    index = jnp.arange(length, dtype=jnp.int32)
    allowed = (segments[:, None] == segments[None, :]) & (index[None, :] <= index[:, None])
    logits = jnp.where(allowed[None], raw * scale, -1e+30)
    probs = jax.nn.softmax(logits, axis=-1)
    mixed = jnp.einsum('hst,td->shd', low(probs), values, precision=lax.Precision.HIGHEST)
    mixed = low(low_back(mixed.reshape(length, HEADS * HEAD_DIM)))
    attn_proj = low_back(matmul(mixed, out_w))
    middle = source + rms_norm(attn_proj, attn_out_gain)
    normed_two = low(rms_norm(middle, ffn_in_gain))
    gate = low_back(matmul(normed_two, gate_w))
    upper = low_back(matmul(normed_two, up_w))
    hidden = low(jax.nn.gelu(gate, approximate=True) * upper)
    ffn_proj = low_back(matmul(hidden, down_w))
    return middle + rms_norm(ffn_proj, ffn_out_gain)

def reference(tokens, segment_ids, w_query, w_key, w_value, w_out, w_gate, w_up, w_down, g_attn_in, g_attn_out, g_ffn_in, g_ffn_out, g_query, g_key, cotangent):
    weights = tuple((item.astype(jnp.float32) for item in (w_query, w_key, w_value, w_out, w_gate, w_up, w_down, g_attn_in, g_attn_out, g_ffn_in, g_ffn_out, g_query, g_key)))
    source = tokens.astype(jnp.float32)
    upstream = cotangent.astype(jnp.float32)

    def forward(inputs, params):

        def one_row(pair):
            return jax.checkpoint(layer_row)(pair[0], pair[1], params)
        return lax.map(one_row, (inputs, segment_ids))
    result, pullback = jax.vjp(forward, source, weights)
    source_grad, weight_grads = pullback(upstream)
    return (result.astype(jnp.bfloat16), source_grad.astype(jnp.bfloat16), weight_grads[0], weight_grads[1], weight_grads[2], weight_grads[3], weight_grads[4], weight_grads[5], weight_grads[6], weight_grads[7], weight_grads[8], weight_grads[9], weight_grads[10], weight_grads[11], weight_grads[12])
```

```python
import jax
import jax.numpy as jnp
from jax import lax
from jax.sharding import PartitionSpec as P

eps = 1e-06


def rms_norm(value, gain):
    return value * lax.rsqrt(jnp.mean(value * value, axis=-1, keepdims=True) + eps) * gain


def positions(segments):
    earlier = (segments[None, :] < segments[:, None]).astype(jnp.int32)
    return jnp.arange(segments.shape[0], dtype=jnp.int32) - jnp.sum(earlier, axis=1)


def rope_tables(where, width):
    half = width // 2
    expo = jnp.arange(half, dtype=jnp.float32) * (2.0 / width)
    freq = jnp.exp(-expo * jnp.log(1000000.0))
    angle = where.astype(jnp.float32)[:, None] * freq[None, :]
    return (jnp.cos(angle), jnp.sin(angle))


def rotate(value, cosine, sine):
    half = value.shape[-1] // 2
    first = value[..., :half]
    second = value[..., half:]
    cosine = cosine[:, None, :]
    sine = sine[:, None, :]
    return jnp.concatenate(
        [first * cosine - second * sine, second * cosine + first * sine], axis=-1
    )


def geglu(gate, upper):
    return jax.nn.gelu(gate, approximate=True) * upper


def across_rows(left, right):
    return lax.dot_general(
        left, right, (((0,), (0,)), ((), ())), preferred_element_type=jnp.float32
    )


def against_cols(left, right):
    return lax.dot_general(
        left, right, (((1,), (1,)), ((), ())), preferred_element_type=jnp.float32
    )


def product(left, right):
    return jnp.dot(left, right, preferred_element_type=jnp.float32)


TEAM = 8
BF16 = jnp.bfloat16
F32 = jnp.float32


class Links:
    def __init__(self, mesh):
        self.nf = mesh.shape["fsdp"]
        self.nr = mesh.shape["rep"]
        assert self.nr == 2 and self.nf % (2 * TEAM) == 0 and self.nf & (self.nf - 1) == 0
        self.teams = self.nf // TEAM
        self.half = self.teams // 2

    def place(self):
        self.f = lax.axis_index("fsdp")
        self.r = lax.axis_index("rep")
        self.lo = self.f % TEAM
        self.hi = self.f // TEAM

    def hop(self, value, *offsets):
        if len(offsets) == 1:
            offsets = offsets * 2
        pairs = [
            (f * self.nr + r, (f ^ offsets[r]) * self.nr + r)
            for f in range(self.nf)
            for r in range(self.nr)
        ]
        return lax.ppermute(value, ("fsdp", "rep"), pairs)

    def swap(self, value):
        return lax.ppermute(value, "rep", [(0, 1), (1, 0)])

    def teams_in_order(self):
        h = self.half
        first = [self.hi ^ (self.r * h + t) for t in range(h)]
        return first + [self.hi ^ ((1 - self.r) * h + t) for t in range(h)]

    def arrange(self, value):
        wide = value.shape[1] // self.teams
        return jnp.concatenate(
            [lax.dynamic_slice_in_dim(value, t * wide, wide, 1) for t in self.teams_in_order()], 1
        )

    def restore(self, value):
        wide = value.shape[1] // self.teams
        out = []
        for natural in range(self.teams):
            t = self.hi ^ natural
            at = jnp.where(t // self.half == self.r, 0, self.half) + t % self.half
            out.append(lax.dynamic_slice_in_dim(value, at * wide, wide, 1))
        return jnp.concatenate(out, 1)


def thirds(rows):
    step = 8 if rows % 8 == 0 else 1
    units = rows // step
    one = -(-units // 3) * step
    two = (rows - one + step) // (2 * step) * step
    return ((0, one), (one, one + two), (one + two, rows))


def spread(links, value):
    hop = links.hop
    got = {0: value, 1: hop(value, 1), 2: hop(value, 2), 4: hop(value, 4)}
    got[3] = hop(got[1], 2)
    got[5] = hop(got[4], 1)
    got[6] = hop(got[2], 4)
    (a0, a1), (b0, b1), (c0, c1) = thirds(value.shape[0])
    got[7] = jnp.concatenate(
        [hop(got[6][a0:a1], 1), hop(got[5][b0:b1], 2), hop(got[3][c0:c1], 4)], 0
    )
    return got


def collect(links, part):
    hop = links.hop
    (a0, a1), (b0, b1), (c0, c1) = thirds(part[0].shape[0])
    low = part[7].astype(BF16)
    to6 = hop(low[a0:a1], 1).astype(F32)
    to5 = hop(low[b0:b1], 2).astype(F32)
    to3 = hop(low[c0:c1], 4).astype(F32)
    six, five, three = (part[o].astype(F32) for o in (6, 5, 3))
    six = jnp.concatenate([six[a0:a1] + to6, six[a1:]], 0).astype(BF16)
    five = jnp.concatenate([five[:b0], five[b0:b1] + to5, five[b1:]], 0).astype(BF16)
    three = jnp.concatenate([three[:c0], three[c0:c1] + to3], 0).astype(BF16)
    two = (part[2].astype(F32) + hop(six, 4).astype(F32)).astype(BF16)
    four = (part[4].astype(F32) + hop(five, 1).astype(F32)).astype(BF16)
    one = (part[1].astype(F32) + hop(three, 2).astype(F32)).astype(BF16)
    return (
        part[0].astype(F32)
        + hop(one, 1).astype(F32)
        + hop(two, 2).astype(F32)
        + hop(four, 4).astype(F32)
    )


def gather_rows(links, shard):
    rows = shard.shape[0]
    teams = []
    for t in range(links.half):
        got = spread(links, links.hop(shard, t * TEAM, (links.half + t) * TEAM))
        block = jnp.zeros((TEAM * rows, shard.shape[1]), shard.dtype)
        for offset in range(TEAM):
            block = lax.dynamic_update_slice_in_dim(
                block, got[offset], (links.lo ^ offset) * rows, 0
            )
        teams.append(block)
    mine = jnp.concatenate(teams, 0)
    return jnp.concatenate([mine, links.swap(mine)], 0)


def scatter_rows(links, term, rows):
    half = term.shape[0] // 2
    mine = term[:half].astype(F32) + links.swap(term[half:].astype(BF16)).astype(F32)
    total = None
    for t in range(links.half):
        block = mine[t * TEAM * rows : (t + 1) * TEAM * rows]
        part = {
            offset: lax.dynamic_slice_in_dim(block, (links.lo ^ offset) * rows, rows, 0)
            for offset in range(TEAM)
        }
        done = collect(links, part).astype(BF16)
        done = links.hop(done, t * TEAM, (links.half + t) * TEAM).astype(F32)
        total = done if total is None else total + done
    total = total.astype(BF16)
    return total.astype(F32) + links.swap(total).astype(F32)


def ffn_cut(width):
    tiles = width // 128
    most = -(-tiles // TEAM)
    fewer = most * TEAM - tiles
    return [most * 128] * (TEAM - fewer) + [(most - 1) * 128] * fewer, most * 128


def ffn_pad(value, sizes, most):
    out, at = [], 0
    for size in sizes:
        out.append(value[:, at : at + size])
        if size < most:
            out.append(jnp.zeros((value.shape[0], most - size), value.dtype))
        at += size
    return jnp.concatenate(out, 1)


def ffn_unpad(value, sizes, most):
    return jnp.concatenate(
        [value[..., i * most : i * most + size] for i, size in enumerate(sizes)], -1
    )


def ffn_fetch(links, shards, most):
    rows = shards[0].shape[0]
    bufs = [jnp.zeros((links.half * TEAM * rows, most), BF16) for _ in shards]
    for t in range(links.half):
        for k in range(TEAM):
            at = (links.lo ^ k) * most
            send = jnp.concatenate(
                [lax.dynamic_slice_in_dim(s, at, most, 1) for s in shards], 0
            )
            got = links.hop(send, t * TEAM + k, (links.half + t) * TEAM + k)
            to = (t * TEAM + (links.lo ^ k)) * rows
            bufs = [
                lax.dynamic_update_slice_in_dim(b, got[i * rows : (i + 1) * rows], to, 0)
                for i, b in enumerate(bufs)
            ]
    mine = jnp.stack(bufs)
    other = links.swap(mine)
    return [jnp.concatenate([mine[i], other[i]], 0) for i in range(len(shards))]


def ffn_return(links, terms, rows, sizes, most):
    half = terms[0].shape[0] // 2
    got = links.swap(jnp.stack([t[half:].astype(BF16) for t in terms]))
    mine = (jnp.stack([t[:half] for t in terms]) + got.astype(F32)).astype(BF16)
    total = None
    for t in range(links.half):
        out = jnp.zeros((len(terms), rows, TEAM * most), BF16)
        for k in range(TEAM):
            block = lax.dynamic_slice_in_dim(mine, (t * TEAM + (links.lo ^ k)) * rows, rows, 1)
            back = links.hop(block, t * TEAM + k, (links.half + t) * TEAM + k)
            out = lax.dynamic_update_slice_in_dim(out, back, (links.lo ^ k) * most, 2)
        total = out if total is None else (total.astype(F32) + out.astype(F32)).astype(BF16)
    total = ffn_unpad(total, sizes, most)
    return total.astype(F32) + links.swap(total).astype(F32)


def everywhere(links, value):
    for offset in [1 << b for b in range(links.nf.bit_length() - 1)]:
        value = value + links.hop(value, offset)
    return value + links.swap(value)


def local(
    links,
    tokens,
    segment_ids,
    w_query,
    w_key,
    w_value,
    w_out,
    w_gate,
    w_up,
    w_down,
    g_attn_in,
    g_attn_out,
    g_ffn_in,
    g_ffn_out,
    g_query,
    g_key,
    cotangent,
):
    links.place()
    rows = w_query.shape[0]
    segments = segment_ids[0]
    head_dim = g_query.shape[0]
    wide_q = w_query.shape[1]
    wide_k = w_key.shape[1]
    heads = wide_q // head_dim
    scale = head_dim ** (-0.5)
    sizes, most = ffn_cut(w_gate.shape[1])

    gains = jnp.stack([g_attn_in, g_attn_out, g_ffn_in, g_ffn_out], 1)
    gains = jnp.pad(gains, ((0, 0), (0, 124)))
    attn_in = gather_rows(links, jnp.concatenate([w_query, w_key, w_value, gains], 1))
    query_w = attn_in[:, :wide_q]
    key_w = attn_in[:, wide_q : wide_q + wide_k]
    value_w = attn_in[:, wide_q + wide_k : wide_q + 2 * wide_k]
    gains = jnp.transpose(attn_in[:, wide_q + 2 * wide_k :].astype(F32))
    attn_in_gain, attn_out_gain, ffn_in_gain, ffn_out_gain = (gains[i] for i in range(4))
    out_flip = gather_rows(links, jnp.transpose(w_out))
    gate_w, up_w = ffn_fetch(
        links, [ffn_pad(w_gate, sizes, most), ffn_pad(w_up, sizes, most)], most
    )
    (down_flip,) = ffn_fetch(links, [ffn_pad(jnp.transpose(w_down), sizes, most)], most)

    source = links.arrange(tokens[0]).astype(F32)
    upstream = links.arrange(cotangent[0]).astype(F32)
    length = source.shape[0]

    normed, attn_in_back = jax.vjp(rms_norm, source, attn_in_gain)
    normed_low = normed.astype(BF16)
    query_proj = product(normed_low, query_w)
    key_proj = product(normed_low, key_w)
    value_low = product(normed_low, value_w).astype(BF16)
    cosine, sine = rope_tables(positions(segments), head_dim)

    def query_path(proj, gain):
        return rotate(rms_norm(proj.reshape(length, heads, head_dim), gain), cosine, sine)

    def key_path(proj, gain):
        return rotate(rms_norm(proj.reshape(length, 1, head_dim), gain), cosine, sine).reshape(
            length, head_dim
        )

    query_rot, query_back = jax.vjp(query_path, query_proj, g_query.astype(F32))
    key_rot, key_back = jax.vjp(key_path, key_proj, g_key.astype(F32))
    query_low = query_rot.astype(BF16)
    key_low = key_rot.astype(BF16)
    index = jnp.arange(length, dtype=jnp.int32)
    allowed = (segments[:, None] == segments[None, :]) & (index[None, :] <= index[:, None])

    raw = jnp.einsum("shd,td->hst", query_low, key_low, preferred_element_type=F32)
    logits = jnp.where(allowed[None], raw * scale, -1e30)
    summit = jnp.max(logits, axis=-1, keepdims=True)
    expo = jnp.exp(logits - summit)
    probs = expo / jnp.sum(expo, axis=-1, keepdims=True)
    probs_low = probs.astype(BF16)
    mixed = jnp.einsum("hst,td->shd", probs_low, value_low, preferred_element_type=F32)
    mixed_low = mixed.reshape(length, heads * head_dim).astype(BF16)
    attn_proj = against_cols(mixed_low, out_flip)
    attn_post, attn_post_back = jax.vjp(rms_norm, attn_proj, attn_out_gain)
    middle = source + attn_post
    normed_two, ffn_in_back = jax.vjp(rms_norm, middle, ffn_in_gain)

    waves = ((0, 1, 2, 4), (3, 5, 6, 7))
    team_in = spread(links, normed_two.astype(BF16))
    ffn_in = [jnp.concatenate([team_in[o] for o in wave], 0) for wave in waves]
    hidden_low, geglu_back, part = [], [], {}
    for wave, value in zip(waves, ffn_in):
        hidden, back = jax.vjp(geglu, product(value, gate_w), product(value, up_w))
        hidden_low.append(hidden.astype(BF16))
        geglu_back.append(back)
        out = against_cols(hidden_low[-1], down_flip)
        for i, o in enumerate(wave):
            part[o] = out[i * length : (i + 1) * length]
    ffn_proj = collect(links, part)
    ffn_post, ffn_post_back = jax.vjp(rms_norm, ffn_proj, ffn_out_gain)
    result = links.restore((middle + ffn_post).astype(BF16))

    ffn_proj_grad, ffn_out_term = ffn_post_back(upstream)
    team_grad = spread(links, ffn_proj_grad.astype(BF16))
    ffn_grad = [jnp.concatenate([team_grad[o] for o in wave], 0) for wave in waves]
    gate_low, upper_low, part = [], [], {}
    for i, (wave, value) in enumerate(zip(waves, ffn_grad)):
        gate_grad, upper_grad = geglu_back[i](product(value, down_flip))
        gate_low.append(gate_grad.astype(BF16))
        upper_low.append(upper_grad.astype(BF16))
        out = against_cols(gate_low[-1], gate_w) + against_cols(upper_low[-1], up_w)
        for j, o in enumerate(wave):
            part[o] = out[j * length : (j + 1) * length]
    normed_two_grad = collect(links, part)
    all_in = jnp.concatenate(ffn_in, 0)
    down_term = across_rows(jnp.concatenate(ffn_grad, 0), jnp.concatenate(hidden_low, 0))
    gate_term = across_rows(all_in, jnp.concatenate(gate_low, 0))
    up_term = across_rows(all_in, jnp.concatenate(upper_low, 0))
    ffn_grads = ffn_return(links, [down_term, gate_term, up_term], rows, sizes, most)

    middle_part, ffn_in_term = ffn_in_back(normed_two_grad)
    middle_grad = upstream + middle_part
    attn_proj_grad, attn_out_term = attn_post_back(middle_grad)
    attn_proj_low = attn_proj_grad.astype(BF16)
    out_term_flip = across_rows(attn_proj_low, mixed_low)
    mixed_grad = product(attn_proj_low, out_flip).astype(BF16).reshape(length, heads, head_dim)
    probs_grad = jnp.einsum("shd,td->hst", mixed_grad, value_low, preferred_element_type=F32)
    value_low_grad = jnp.einsum(
        "hst,shd->td", probs_low, mixed_grad, preferred_element_type=F32
    ).astype(BF16)
    row_dot = jnp.sum(probs * probs_grad, axis=-1, keepdims=True)
    score_grad = (probs * (probs_grad - row_dot) * scale).astype(BF16)
    query_rot_grad = jnp.einsum("hst,td->shd", score_grad, key_low, preferred_element_type=F32)
    key_rot_grad = jnp.einsum("hst,shd->td", score_grad, query_low, preferred_element_type=F32)
    query_rot_grad = query_rot_grad.astype(BF16).astype(F32)
    key_rot_grad = key_rot_grad.astype(BF16).astype(F32)
    query_proj_grad, query_gain_term = query_back(query_rot_grad)
    key_proj_grad, key_gain_term = key_back(key_rot_grad)
    proj_low = jnp.concatenate(
        [query_proj_grad.astype(BF16), key_proj_grad.astype(BF16), value_low_grad], 1
    )
    proj_term = across_rows(normed_low, proj_low)
    normed_grad = against_cols(proj_low, attn_in[:, : wide_q + 2 * wide_k])
    source_part, attn_in_term = attn_in_back(normed_grad)
    source_grad = links.restore((middle_grad + source_part).astype(BF16))

    gain_terms = jnp.stack([attn_in_term, attn_out_term, ffn_in_term, ffn_out_term], 1)
    gain_terms = jnp.pad(gain_terms, ((0, 0), (0, 124)))
    out_shard = scatter_rows(links, out_term_flip, rows)
    shard = scatter_rows(links, jnp.concatenate([proj_term, gain_terms], 1), rows)
    gain_sums = everywhere(links, jnp.stack([query_gain_term, key_gain_term]))
    gain_shard = shard[:, wide_q + 2 * wide_k :]
    return (
        result[None],
        source_grad[None],
        shard[:, :wide_q],
        shard[:, wide_q : wide_q + wide_k],
        shard[:, wide_q + wide_k : wide_q + 2 * wide_k],
        jnp.transpose(out_shard),
        ffn_grads[1],
        ffn_grads[2],
        jnp.transpose(ffn_grads[0]),
        gain_shard[:, 0],
        gain_shard[:, 1],
        gain_shard[:, 2],
        gain_shard[:, 3],
        gain_sums[0],
        gain_sums[1],
    )


def solution(mesh):
    links = Links(mesh)
    rows = P(("fsdp", "rep"), None, None)
    placed = (
        rows,
        P(("fsdp", "rep"), None),
        P("fsdp", None),
        P("fsdp", None),
        P("fsdp", None),
        P(None, "fsdp"),
        P("fsdp", None),
        P("fsdp", None),
        P(None, "fsdp"),
        P("fsdp"),
        P("fsdp"),
        P("fsdp"),
        P("fsdp"),
        P(),
        P(),
        rows,
    )
    return jax.shard_map(
        lambda *arrays: local(links, *arrays),
        mesh=mesh,
        in_specs=placed,
        out_specs=(rows, rows) + placed[2:13] + (P(), P()),
        check_vma=False,
    )
```

```python
import functools

import jax
import jax.numpy as jnp
from jax import lax
from jax.experimental import pallas as pl
from jax.experimental.pallas import tpu as pltpu
from jax.sharding import PartitionSpec as P

eps = 1e-06


def rms_norm(value, gain):
    return value * lax.rsqrt(jnp.mean(value * value, axis=-1, keepdims=True) + eps) * gain


def positions(segments):
    earlier = (segments[None, :] < segments[:, None]).astype(jnp.int32)
    return jnp.arange(segments.shape[0], dtype=jnp.int32) - jnp.sum(earlier, axis=1)


def rope_tables(where, width):
    half = width // 2
    expo = jnp.arange(half, dtype=jnp.float32) * (2.0 / width)
    freq = jnp.exp(-expo * jnp.log(1000000.0))
    angle = where.astype(jnp.float32)[:, None] * freq[None, :]
    return (jnp.cos(angle), jnp.sin(angle))


def rotate(value, cosine, sine):
    half = value.shape[-1] // 2
    first = value[..., :half]
    second = value[..., half:]
    cosine = cosine[:, None, :]
    sine = sine[:, None, :]
    return jnp.concatenate(
        [first * cosine - second * sine, second * cosine + first * sine], axis=-1
    )


def geglu(gate, upper):
    return jax.nn.gelu(gate, approximate=True) * upper


def across_rows(left, right):
    return lax.dot_general(
        left, right, (((0,), (0,)), ((), ())), preferred_element_type=jnp.float32
    )


def against_cols(left, right):
    return lax.dot_general(
        left, right, (((1,), (1,)), ((), ())), preferred_element_type=jnp.float32
    )


def product(left, right):
    return jnp.dot(left, right, preferred_element_type=jnp.float32)


TEAM = 8
BF16 = jnp.bfloat16
F32 = jnp.float32


class Links:
    def __init__(self, mesh):
        self.nf = mesh.shape["fsdp"]
        self.nr = mesh.shape["rep"]
        assert self.nr == 2 and self.nf % (2 * TEAM) == 0 and self.nf & (self.nf - 1) == 0
        self.teams = self.nf // TEAM
        self.half = self.teams // 2

    def place(self):
        self.f = lax.axis_index("fsdp")
        self.r = lax.axis_index("rep")
        self.lo = self.f % TEAM
        self.hi = self.f // TEAM

    def seat(self, number):
        first, second = role(number)
        return self.lo ^ jnp.where(self.r == 0, first, second)

    def hop(self, value, *offsets):
        if len(offsets) == 1:
            offsets = offsets * 2
        pairs = [
            (f * self.nr + r, (f ^ offsets[r]) * self.nr + r)
            for f in range(self.nf)
            for r in range(self.nr)
        ]
        return lax.ppermute(value, ("fsdp", "rep"), pairs)

    def swap(self, value):
        return lax.ppermute(value, "rep", [(0, 1), (1, 0)])

    def teams_in_order(self):
        h = self.half
        first = [self.hi ^ (self.r * h + t) for t in range(h)]
        return first + [self.hi ^ ((1 - self.r) * h + t) for t in range(h)]

    def arrange(self, value):
        wide = value.shape[1] // self.teams
        return jnp.concatenate(
            [lax.dynamic_slice_in_dim(value, t * wide, wide, 1) for t in self.teams_in_order()], 1
        )

    def restore(self, value):
        wide = value.shape[1] // self.teams
        out = []
        for natural in range(self.teams):
            t = self.hi ^ natural
            at = jnp.where(t // self.half == self.r, 0, self.half) + t % self.half
            out.append(lax.dynamic_slice_in_dim(value, at * wide, wide, 1))
        return jnp.concatenate(out, 1)


ROLE_BITS = ((1, 2, 4), (2, 4, 1))


def role(number):
    return tuple(
        sum(bits[i] for i in range(3) if number >> i & 1) for bits in ROLE_BITS
    )


def tie(value, *others):
    return lax.optimization_barrier((value,) + others)[0]


class Side:
    def __init__(self, stream):
        self.stream = stream
        self.last = None

    def step(self, value):
        self.last = next(self.stream, self.last)
        return tie(value, self.last)

    def rest(self):
        for self.last in self.stream:
            pass
        return self.last


def spread(links, value, side=None):
    def hop(block, number):
        return links.hop(block, *role(number))

    got = {0: value, 1: hop(value, 1), 2: hop(value, 2), 4: hop(value, 4)}
    if side:
        got[1] = side.step(got[1])
    got[3] = hop(got[1], 2)
    got[5] = hop(got[4], 1)
    got[6] = hop(got[2], 4)
    if side:
        got[6] = side.step(got[6])
    got[7] = hop(got[6], 1)
    return got


def collect(links, part, side=None):
    def add(number, block, by):
        return part[number].astype(F32) + links.hop(block.astype(BF16), *role(by)).astype(F32)

    six = add(6, part[7], 1)
    four = add(4, part[5], 1)
    one = add(1, part[3], 2)
    if side:
        six = side.step(six)
    two = add(2, six, 4)
    if side:
        two = side.step(two)
    return (
        add(0, one, 1)
        + links.hop(four.astype(BF16), *role(4)).astype(F32)
        + links.hop(two.astype(BF16), *role(2)).astype(F32)
    )


def gather_rows(links, crossed, side):
    rows = crossed[0].shape[0]
    teams = []
    for shard in crossed:
        got = spread(links, shard, side)
        block = jnp.zeros((TEAM, rows, shard.shape[1]), shard.dtype)
        for number in range(TEAM):
            block = lax.dynamic_update_slice_in_dim(
                block, got[number][None], links.seat(number), 0
            )
        teams.append(block.reshape(TEAM * rows, -1))
    mine = jnp.concatenate(teams, 0)
    return jnp.concatenate([mine, links.swap(side.step(mine))], 0)


def scatter_rows(links, mine, other, rows, side):
    mine = mine + links.swap(side.step(other)).astype(F32)
    total = None
    for t in range(links.half):
        block = mine[t * TEAM * rows : (t + 1) * TEAM * rows]
        part = {
            number: lax.dynamic_slice_in_dim(block, links.seat(number) * rows, rows, 0)
            for number in range(TEAM)
        }
        done = side.step(collect(links, part, side).astype(BF16))
        done = links.hop(done, t * TEAM, (links.half + t) * TEAM).astype(F32)
        total = done if total is None else total + done
    total = side.step(total.astype(BF16))
    return total.astype(F32) + links.swap(total).astype(F32)


def ffn_cut(width):
    tiles = width // 128
    most = -(-tiles // TEAM)
    fewer = most * TEAM - tiles
    return [most * 128] * (TEAM - fewer) + [(most - 1) * 128] * fewer, most * 128


def ffn_pad(value, sizes, most):
    out, at = [], 0
    for size in sizes:
        out.append(value[:, at : at + size])
        if size < most:
            out.append(jnp.zeros((value.shape[0], most - size), value.dtype))
        at += size
    return jnp.concatenate(out, 1)


def ffn_unpad(value, sizes, most):
    return jnp.concatenate(
        [value[..., i * most : i * most + size] for i, size in enumerate(sizes)], -1
    )


def ffn_fetch(links, shards, most, after):
    rows = shards[0].shape[0]
    count = len(shards)
    whole = [jnp.zeros((links.nf, rows, most), BF16) for _ in shards]
    half = links.half * TEAM
    arrived, pending = [after], []

    def put(seat, piece):
        for i in range(count):
            whole[i] = lax.dynamic_update_slice_in_dim(
                whole[i], piece[i : i + 1], seat, 0
            )

    steps = [(t, k) for t in range(links.half) for k in range(TEAM)]
    for n, (t, k) in enumerate(steps):
        at = (links.lo ^ k) * most
        send = jnp.stack([lax.dynamic_slice_in_dim(s, at, most, 1) for s in shards])
        send = tie(send, arrived[max(0, n - 1)])
        got = links.hop(send, t * TEAM + k, (links.half + t) * TEAM + k)
        arrived.append(got)
        put(t * TEAM + (links.lo ^ k), got)
        pending.append((t * TEAM + (links.lo ^ k), got))
        if len(pending) == len(steps) // 2:
            other = links.swap(jnp.stack([p for _, p in pending]))
            for j, (seat, _) in enumerate(pending):
                put(half + seat, other[j])
            pending = []
        yield got
    yield [w.reshape(links.nf * rows, most) for w in whole]


def ffn_return(links, terms, rows, sizes, most):
    half = terms[0].shape[0] // 2
    got = links.swap(jnp.stack([t[half:].astype(BF16) for t in terms]))
    yield got
    mine = (jnp.stack([t[:half] for t in terms]) + got.astype(F32)).astype(BF16)
    total = None
    arrived = [mine, mine]
    for t in range(links.half):
        out = jnp.zeros((len(terms), rows, TEAM * most), BF16)
        for k in range(TEAM):
            block = lax.dynamic_slice_in_dim(mine, (t * TEAM + (links.lo ^ k)) * rows, rows, 1)
            back = links.hop(
                tie(block, arrived[-2]), t * TEAM + k, (links.half + t) * TEAM + k
            )
            arrived.append(back)
            out = lax.dynamic_update_slice_in_dim(out, back, (links.lo ^ k) * most, 2)
            yield back
        total = out if total is None else (total.astype(F32) + out.astype(F32)).astype(BF16)
    total = ffn_unpad(total, sizes, most)
    yield total.astype(F32) + links.swap(total).astype(F32)


def everywhere(links, value):
    for offset in [1 << b for b in range(links.nf.bit_length() - 1)]:
        value = value + links.hop(value, offset)
    return value + links.swap(value)


def norm_back(value, gain, grad):
    inv = lax.rsqrt(jnp.mean(value * value, axis=-1, keepdims=True) + eps)
    scaled = grad * gain
    mean = jnp.mean(scaled * value, axis=-1, keepdims=True)
    back = scaled * inv - value * (inv * inv * inv * mean)
    return back, jnp.sum(grad * (value * inv), axis=0, keepdims=True)


def turn(value, cosine, sine):
    half = value.shape[-1] // 2
    first, second = value[:, :half], value[:, half:]
    return jnp.concatenate([first * cosine - second * sine, second * cosine + first * sine], 1)


def attend_kernel(
    heads,
    x_ref,
    w_ref,
    gq_ref,
    gk_ref,
    cos_ref,
    sin_ref,
    seg_row_ref,
    seg_col_ref,
    h1_ref,
    proj_ref,
    q_ref,
    k_ref,
    v_ref,
    p_ref,
    a_ref,
    o_ref,
    x2_ref,
    h2_ref,
    gains_ref,
):
    dim = k_ref.shape[1]
    wide_q = heads * dim
    wide_p = wide_q + 2 * dim
    length = x_ref.shape[0]
    source = x_ref[...].astype(F32)
    gains = jnp.transpose(w_ref[:, wide_p : wide_p + 128].astype(F32))
    gains_ref[...] = gains[:8]
    h1 = rms_norm(source, gains[0:1]).astype(BF16)
    h1_ref[...] = h1
    proj = product(h1, w_ref[:, :wide_p])
    proj_ref[...] = proj[:, : wide_q + dim]
    value = proj[:, wide_q + dim :].astype(BF16)
    v_ref[...] = value
    cosine, sine = cos_ref[...], sin_ref[...]
    key = turn(rms_norm(proj[:, wide_q : wide_q + dim], gk_ref[...]), cosine, sine).astype(BF16)
    k_ref[...] = key
    row = lax.broadcasted_iota(jnp.int32, (length, length), 0)
    col = lax.broadcasted_iota(jnp.int32, (length, length), 1)
    allowed = (seg_col_ref[...] == seg_row_ref[...]) & (col <= row)
    for h in range(heads):
        cut = slice(h * dim, (h + 1) * dim)
        query = turn(rms_norm(proj[:, cut], gq_ref[...]), cosine, sine).astype(BF16)
        q_ref[:, cut] = query
        logits = jnp.where(allowed, against_cols(query, key) * dim ** (-0.5), -1e30)
        expo = jnp.exp(logits - jnp.max(logits, axis=-1, keepdims=True))
        probs = expo / jnp.sum(expo, axis=-1, keepdims=True)
        p_ref[h] = probs
        a_ref[:, cut] = product(probs.astype(BF16), value).astype(BF16)
    out = against_cols(a_ref[...], w_ref[:, wide_p + 128 :])
    o_ref[...] = out
    middle = source + rms_norm(out, gains[1:2])
    x2_ref[...] = middle
    h2_ref[...] = rms_norm(middle, gains[2:3]).astype(BF16)


def after_kernel(f_ref, x2_ref, c_ref, gains_ref, result_ref, df_ref, term_ref):
    value = f_ref[...]
    gain = gains_ref[3:4]
    result_ref[...] = (x2_ref[...] + rms_norm(value, gain)).astype(BF16)
    back, term = norm_back(value, gain, c_ref[...].astype(F32))
    df_ref[...] = back.astype(BF16)
    term_ref[...] = term


def attend_back_kernel(
    heads,
    dh2_ref,
    c_ref,
    x_ref,
    x2_ref,
    o_ref,
    gains_ref,
    ffn_out_ref,
    w_ref,
    h1_ref,
    proj_ref,
    q_ref,
    k_ref,
    v_ref,
    p_ref,
    a_ref,
    gq_ref,
    gk_ref,
    cos_ref,
    sin_ref,
    grad_ref,
    mine_ref,
    other_ref,
    gain_ref,
    low_ref,
):
    dim = k_ref.shape[1]
    wide_q = heads * dim
    wide_p = wide_q + 2 * dim
    half = mine_ref.shape[0]
    scale = dim ** (-0.5)
    gains = gains_ref[...]
    back, ffn_in_term = norm_back(x2_ref[...], gains[2:3], dh2_ref[...])
    middle = c_ref[...].astype(F32) + back
    out_back, attn_out_term = norm_back(o_ref[...], gains[1:2], middle)
    out_low = out_back.astype(BF16)
    mixed = product(out_low, w_ref[:, wide_p + 128 :]).astype(BF16)
    key, value = k_ref[...], v_ref[...]
    cosine, sine = cos_ref[...], sin_ref[...]
    key_back, value_back, query_gain = 0.0, 0.0, 0.0
    for h in range(heads):
        cut = slice(h * dim, (h + 1) * dim)
        probs = p_ref[h]
        mixed_h = mixed[:, cut]
        probs_back = against_cols(mixed_h, value)
        value_back = value_back + across_rows(probs.astype(BF16), mixed_h)
        row_dot = jnp.sum(probs * probs_back, axis=-1, keepdims=True)
        score = (probs * (probs_back - row_dot) * scale).astype(BF16)
        key_back = key_back + across_rows(score, q_ref[:, cut])
        query_back = product(score, key).astype(BF16).astype(F32)
        query_back, term = norm_back(
            proj_ref[:, cut], gq_ref[...], turn(query_back, cosine, -sine)
        )
        query_gain = query_gain + term
        low_ref[:, cut] = query_back.astype(BF16)
    key_back = key_back.astype(BF16).astype(F32)
    key_back, key_gain = norm_back(
        proj_ref[:, wide_q : wide_q + dim], gk_ref[...], turn(key_back, cosine, -sine)
    )
    low_ref[:, wide_q : wide_q + dim] = key_back.astype(BF16)
    low_ref[:, wide_q + dim :] = value_back.astype(BF16)
    gain_ref[...] = jnp.concatenate([query_gain, key_gain, jnp.zeros((6, dim), F32)], 0)
    low = low_ref[...]
    source = x_ref[...].astype(F32)
    back, attn_in_term = norm_back(source, gains[0:1], against_cols(low, w_ref[:, :wide_p]))
    grad_ref[...] = (middle + back).astype(BF16)
    terms = jnp.concatenate([attn_in_term, attn_out_term, ffn_in_term, ffn_out_ref[...]], 0)
    terms = jnp.concatenate([terms, jnp.zeros((124, terms.shape[1]), F32)], 0)
    terms = jnp.transpose(terms)
    mine_ref[:, wide_p : wide_p + 128] = terms[:half]
    other_ref[:, wide_p : wide_p + 128] = terms[half:].astype(BF16)
    h1 = h1_ref[...]
    mine_ref[:, :wide_p] = across_rows(h1[:, :half], low)
    other_ref[:, :wide_p] = across_rows(h1[:, half:], low).astype(BF16)
    mine_ref[:, wide_p + 128 :] = across_rows(out_low[:, :half], a_ref[...])
    other_ref[:, wide_p + 128 :] = across_rows(out_low[:, half:], a_ref[...]).astype(BF16)


def call(kernel, outs, flops, scratch, *arrays):
    size = sum(a.size * a.dtype.itemsize for a in arrays)
    return pl.pallas_call(
        kernel,
        out_shape=[jax.ShapeDtypeStruct(shape, kind) for shape, kind in outs],
        scratch_shapes=scratch,
        cost_estimate=pl.CostEstimate(flops=flops, bytes_accessed=size, transcendentals=0),
        compiler_params=pltpu.CompilerParams(vmem_limit_bytes=40 << 20),
    )(*arrays)


def local(
    links,
    tokens,
    segment_ids,
    w_query,
    w_key,
    w_value,
    w_out,
    w_gate,
    w_up,
    w_down,
    g_attn_in,
    g_attn_out,
    g_ffn_in,
    g_ffn_out,
    g_query,
    g_key,
    cotangent,
):
    links.place()
    rows = w_query.shape[0]
    segments = segment_ids[0]
    head_dim = g_query.shape[0]
    wide_q = w_query.shape[1]
    wide_k = w_key.shape[1]
    wide_p = wide_q + 2 * wide_k
    heads = wide_q // head_dim
    sizes, most = ffn_cut(w_gate.shape[1])
    length, width = tokens.shape[1:]

    gains = jnp.stack([g_attn_in, g_attn_out, g_ffn_in, g_ffn_out], 1)
    gains = jnp.pad(gains, ((0, 0), (0, 124)))
    shard = jnp.concatenate([w_query, w_key, w_value, gains, jnp.transpose(w_out)], 1)
    crossed = [
        links.hop(shard, t * TEAM, (links.half + t) * TEAM) for t in range(links.half)
    ]
    padded = [ffn_pad(w, sizes, most) for w in (w_gate, w_up, jnp.transpose(w_down))]
    fetch = Side(ffn_fetch(links, padded, most, crossed[-1]))
    weights = gather_rows(links, crossed, fetch)

    source = links.arrange(tokens[0])
    upstream = links.arrange(cotangent[0])
    cosine, sine = rope_tables(positions(segments), head_dim)
    gain_q = g_query.astype(F32)[None]
    gain_k = g_key.astype(F32)[None]
    normed, proj, query, key, value, probs, mixed, out, middle, normed_two, gains = call(
        functools.partial(attend_kernel, heads),
        [
            ((length, width), BF16),
            ((length, wide_q + wide_k), F32),
            ((length, wide_q), BF16),
            ((length, wide_k), BF16),
            ((length, wide_k), BF16),
            ((heads, length, length), F32),
            ((length, wide_q), BF16),
            ((length, width), F32),
            ((length, width), F32),
            ((length, width), BF16),
            ((8, width), F32),
        ],
        2 * length * weights.size,
        [],
        source,
        fetch.step(weights),
        gain_q,
        gain_k,
        cosine,
        sine,
        segments[None],
        segments[:, None],
    )

    waves = ((0, 1, 2, 4), (3, 5, 6, 7))
    team_in = spread(links, fetch.step(normed_two), fetch)
    gate_w, up_w, down_flip = fetch.rest()
    ffn_in = [jnp.concatenate([team_in[o] for o in wave], 0) for wave in waves]
    hidden_low, geglu_back, part = [], [], {}
    for wave, block in zip(waves, ffn_in):
        hidden, back = jax.vjp(geglu, product(block, gate_w), product(block, up_w))
        hidden_low.append(hidden.astype(BF16))
        geglu_back.append(back)
        partial = against_cols(hidden_low[-1], down_flip)
        for i, o in enumerate(wave):
            part[o] = partial[i * length : (i + 1) * length]
    ffn_proj = collect(links, part)
    result, ffn_proj_grad, ffn_out_term = call(
        after_kernel,
        [((length, width), BF16), ((length, width), BF16), ((1, width), F32)],
        length * width * 20,
        [],
        ffn_proj,
        middle,
        upstream,
        gains,
    )

    team_grad = spread(links, ffn_proj_grad)
    ffn_grad = [jnp.concatenate([team_grad[o] for o in wave], 0) for wave in waves]
    gate_low, upper_low, part = [], [], {}
    for i, (wave, block) in enumerate(zip(waves, ffn_grad)):
        gate_grad, upper_grad = geglu_back[i](product(block, down_flip))
        gate_low.append(gate_grad.astype(BF16))
        upper_low.append(upper_grad.astype(BF16))
        partial = against_cols(gate_low[-1], gate_w) + against_cols(upper_low[-1], up_w)
        for j, o in enumerate(wave):
            part[o] = partial[j * length : (j + 1) * length]
    all_in = jnp.concatenate(ffn_in, 0)
    down_term = across_rows(jnp.concatenate(ffn_grad, 0), jnp.concatenate(hidden_low, 0))
    gate_term = across_rows(all_in, jnp.concatenate(gate_low, 0))
    up_term = across_rows(all_in, jnp.concatenate(upper_low, 0))
    back = Side(ffn_return(links, [down_term, gate_term, up_term], rows, sizes, most))
    normed_two_grad = collect(links, part, back)

    half = width // 2
    wide_w = weights.shape[1]
    source_grad, mine, other, gain_terms = call(
        functools.partial(attend_back_kernel, heads),
        [
            ((length, width), BF16),
            ((half, wide_w), F32),
            ((half, wide_w), BF16),
            ((8, head_dim), F32),
        ],
        4 * length * weights.size,
        [pltpu.VMEM((length, wide_p), BF16)],
        back.step(normed_two_grad),
        upstream,
        source,
        middle,
        out,
        gains,
        ffn_out_term,
        weights,
        normed,
        proj,
        query,
        key,
        value,
        probs,
        mixed,
        gain_q,
        gain_k,
        cosine,
        sine,
    )
    shard = scatter_rows(links, mine, other, rows, back)
    gain_sums = everywhere(links, gain_terms)
    gain_shard = shard[:, wide_p : wide_p + 128]
    down_grad, gate_grad, up_grad = back.rest()
    return (
        links.restore(result)[None],
        links.restore(source_grad)[None],
        shard[:, :wide_q],
        shard[:, wide_q : wide_q + wide_k],
        shard[:, wide_q + wide_k : wide_p],
        jnp.transpose(shard[:, wide_p + 128 :]),
        gate_grad,
        up_grad,
        jnp.transpose(down_grad),
        gain_shard[:, 0],
        gain_shard[:, 1],
        gain_shard[:, 2],
        gain_shard[:, 3],
        gain_sums[0],
        gain_sums[1],
    )


def solution(mesh):
    links = Links(mesh)
    rows = P(("fsdp", "rep"), None, None)
    placed = (
        rows,
        P(("fsdp", "rep"), None),
        P("fsdp", None),
        P("fsdp", None),
        P("fsdp", None),
        P(None, "fsdp"),
        P("fsdp", None),
        P("fsdp", None),
        P(None, "fsdp"),
        P("fsdp"),
        P("fsdp"),
        P("fsdp"),
        P("fsdp"),
        P(),
        P(),
        rows,
    )
    return jax.shard_map(
        lambda *arrays: local(links, *arrays),
        mesh=mesh,
        in_specs=placed,
        out_specs=(rows, rows) + placed[2:13] + (P(), P()),
        check_vma=False,
    )
```

```python
import functools

import jax
import jax.numpy as jnp
from jax import lax
from jax.experimental import pallas as pl
from jax.experimental.pallas import tpu as pltpu
from jax.sharding import PartitionSpec as P

eps = 1e-06


def rms_norm(value, gain):
    return value * lax.rsqrt(jnp.mean(value * value, axis=-1, keepdims=True) + eps) * gain


def positions(segments):
    earlier = (segments[None, :] < segments[:, None]).astype(jnp.int32)
    return jnp.arange(segments.shape[0], dtype=jnp.int32) - jnp.sum(earlier, axis=1)


def rope_tables(where, width):
    half = width // 2
    expo = jnp.arange(half, dtype=jnp.float32) * (2.0 / width)
    freq = jnp.exp(-expo * jnp.log(1000000.0))
    angle = where.astype(jnp.float32)[:, None] * freq[None, :]
    return (jnp.cos(angle), jnp.sin(angle))


def rotate(value, cosine, sine):
    half = value.shape[-1] // 2
    first = value[..., :half]
    second = value[..., half:]
    cosine = cosine[:, None, :]
    sine = sine[:, None, :]
    return jnp.concatenate(
        [first * cosine - second * sine, second * cosine + first * sine], axis=-1
    )


def geglu(gate, upper):
    return jax.nn.gelu(gate, approximate=True) * upper


def across_rows(left, right):
    return lax.dot_general(
        left, right, (((0,), (0,)), ((), ())), preferred_element_type=jnp.float32
    )


def against_cols(left, right):
    return lax.dot_general(
        left, right, (((1,), (1,)), ((), ())), preferred_element_type=jnp.float32
    )


def product(left, right):
    return jnp.dot(left, right, preferred_element_type=jnp.float32)


TEAM = 8
BF16 = jnp.bfloat16
F32 = jnp.float32


class Links:
    def __init__(self, mesh):
        self.nf = mesh.shape["fsdp"]
        self.nr = mesh.shape["rep"]
        assert self.nr == 2 and self.nf % (2 * TEAM) == 0 and self.nf & (self.nf - 1) == 0
        self.teams = self.nf // TEAM
        self.half = self.teams // 2

    def place(self):
        self.f = lax.axis_index("fsdp")
        self.r = lax.axis_index("rep")
        self.lo = self.f % TEAM
        self.hi = self.f // TEAM
        side = self.hi // self.half
        self.mine = side ^ self.r
        self.other = side ^ (1 - self.r)

    def seat(self, number):
        first, second = role(number)
        return self.lo ^ jnp.where(self.r == 0, first, second)

    def go(self, value, how):
        if how is None:
            return lax.ppermute(value, "rep", [(0, 1), (1, 0)])
        pairs = [
            (f * self.nr + r, (f ^ how[r]) * self.nr + r)
            for f in range(self.nf)
            for r in range(self.nr)
            if how[r] is not None
        ]
        return lax.ppermute(value, ("fsdp", "rep"), pairs)

    def both(self, offset):
        return offset, offset

    def cross(self, team):
        return team * TEAM, (self.half + team) * TEAM

    def half_rows(self, value, side, axis=0):
        size = value.shape[axis] // 2
        return lax.dynamic_slice_in_dim(value, side * size, size, axis)

    def blocks(self, order):
        return [
            (
                (t * TEAM + k, (self.half + t) * TEAM + k),
                ((self.hi ^ t) % self.half) * TEAM + (self.lo ^ k),
            )
            for t in range(self.half)
            for k in order
        ]


ROLE_BITS = ((1, 2, 4), (2, 4, 1))


def role(number):
    return tuple(
        sum(bits[i] for i in range(3) if number >> i & 1) for bits in ROLE_BITS
    )


class Stream:
    def __init__(self, sends):
        self.sends = list(sends)
        self.got = []
        self.seen = 0

    def oldest(self, count):
        return self.got[self.seen : self.seen + count]

    def waited(self, values):
        self.got[self.seen : self.seen + len(values)] = values
        self.seen += len(values)

    def next(self, count):
        out, self.sends = self.sends[:count], self.sends[count:]
        return [(value() if callable(value) else value, how) for value, how in out]

    def sent(self, values):
        self.got += values


class Held:
    def __init__(self, arrays, steps):
        self.arrays = arrays
        self.steps = steps

    def before(self, n):
        self.arrays = self.steps[n](self.arrays)
        return self.arrays


def everywhere(links, value):
    value = value.astype(F32)
    value = value + links.go(value, None)
    for bit in range(links.nf.bit_length() - 1):
        value = value + links.go(value, links.both(1 << bit))
    return value


def point(links, waits, sends, *streams):
    olds = [stream.oldest(w) for stream, w, _ in streams]
    waits, olds, values = lax.optimization_barrier((waits, olds, [v for v, _ in sends]))
    for (stream, _, _), old in zip(streams, olds):
        stream.waited(old)
    mores = [stream.next(s) for stream, _, s in streams]
    flat = [v for more in mores for v, _ in more]
    waits, olds, values, flat = lax.optimization_barrier((waits, olds, values, flat))
    for (stream, _, _), old in zip(streams, olds):
        stream.got[stream.seen - len(old) : stream.seen] = old
    got = [links.go(v, how) for v, (_, how) in zip(values, sends)]
    flat = iter(flat)
    for (stream, _, _), more in zip(streams, mores):
        stream.sent([links.go(next(flat), how) for _, how in more])
    return waits, got


def spread(links, value, plans=((), (), ()), held=None):
    by = {n: role(n) for n in (1, 2, 4)}

    def step(n, waits, sends):
        (waits, made), got = point(links, [waits, held.before(n) if held else []], sends, *plans[n])
        if held:
            held.arrays = made
        return waits, got

    _, (one, two, four) = step(0, [], [(value, by[n]) for n in (1, 2, 4)])
    yield {0: value, 1: one, 2: two, 4: four}
    sends = [(one, by[2]), (four, by[1]), (two, by[4])]
    near, (three, five, six) = step(1, [one, two, four], sends)
    far, (seven,) = step(2, [three, five], [(six, by[1])])
    yield {3: far[0], 5: far[1], 6: six}
    yield {7: seven}


class Sum:
    def __init__(self, value, col):
        self.value = value
        self.col = col

    def put(self, block):
        rows, cols = self.value.shape
        row = lax.broadcasted_iota(jnp.int32, block.shape, 0)
        col = lax.broadcasted_iota(jnp.int32, block.shape, 1)
        own = (row < rows) & (col >= self.col) & (col < self.col + cols)
        edges = ((0, block.shape[0] - rows), (self.col, block.shape[1] - self.col - cols))
        return jnp.where(own, jnp.pad(self.value, edges), block)

    def add(self, block):
        rows, cols = self.value.shape
        other = block[:rows, self.col : self.col + cols]
        self.value = (self.value.astype(F32) + other.astype(F32)).astype(BF16)


def collect(links, parts, plans, extra=None, hook=None):
    by = {n: role(n) for n in (1, 2, 4)}

    def add(part, number, block):
        return part[number].astype(F32) + block.astype(F32)

    def carry(blocks):
        return [extra.put(b) if extra and i == 0 else b for i, b in enumerate(blocks)]

    def carried(blocks):
        if extra:
            extra.add(blocks[0])

    sends = carry([p[7].astype(BF16) for p in parts])
    _, got = point(links, [], [(v, by[1]) for v in sends], *plans[0])
    carried(got)
    sixes = carry([add(p, 6, v).astype(BF16) for p, v in zip(parts, got)])
    sends = []
    for part, six in zip(parts, sixes):
        sends += [(six, by[4]), (part[5].astype(BF16), by[1]), (part[3].astype(BF16), by[2])]
    if hook:
        sends = hook(sends)
    _, got = point(links, [], sends, *plans[1])
    carried(got)
    twos = carry([add(p, 2, got[3 * i]).astype(BF16) for i, p in enumerate(parts)])
    sends = []
    for i, (part, two) in enumerate(zip(parts, twos)):
        sends.append((two, by[2]))
        for n, j in ((4, 1), (1, 2)):
            sends.append((add(part, n, got[3 * i + j]).astype(BF16), by[n]))
    _, got = point(links, [], sends, *plans[2])
    carried(got)
    return [(p[0], *got[3 * i : 3 * i + 3]) for i, p in enumerate(parts)]


def ffn_cut(width):
    tiles = width // 128
    most = -(-tiles // TEAM)
    return TEAM - (most * TEAM - tiles), most * 128


def ffn_window(seat, width):
    full, most = ffn_cut(width)
    start = seat * most - jnp.maximum(seat - full, 0) * 128
    at = jnp.minimum(start, width - most)
    size = jnp.where(seat < full, most, most - 128)
    return at, start - at, start - at + size


def ffn_pack_kernel(seat_ref, gate_ref, up_ref, down_ref, *out_refs):
    width = gate_ref.shape[1]
    rows, most = out_refs[0].shape[1:]
    col = lax.broadcasted_iota(jnp.int32, (rows, most), 1)
    for k in range(TEAM):
        at, first, end = ffn_window(seat_ref[0] ^ k, width)
        own = (col >= first) & (col < end)
        for i, ref in enumerate((gate_ref, up_ref, down_ref)):
            block = ref[:, pl.ds(pl.multiple_of(at, 128), most)].astype(F32)
            out_refs[k][i] = jnp.where(own, block, 0.0).astype(BF16)


def ffn_unpack_kernel(order, seat_ref, *refs):
    block_refs, other_refs, out_refs = refs[:TEAM], refs[TEAM:-3], refs[-3:]
    width = out_refs[0].shape[1]
    most = block_refs[0].shape[2]
    others = [ref.at[n] for ref in other_refs for n in range(ref.shape[0])]
    less = most - 128

    def place(k, block, other):
        at, first, end = ffn_window(seat_ref[0] ^ k, width)
        start = pl.multiple_of(at + first, 128)
        for skip, size in ((0, most), (0, less), (128, less)):

            @pl.when((end - first == size) & (first == skip))
            def _(skip=skip, size=size):
                cut = slice(skip, skip + size)
                for i, out_ref in enumerate(out_refs):
                    value = block[i, :, cut].astype(F32) + other[i, :, cut].astype(F32)
                    out_ref[:, pl.ds(start, size)] = value

    for k, block, other in zip(order, block_refs, others):
        place(k, block, other)


def pack_kernel(*refs):
    ins, shard_ref = refs[:-1], refs[-1]
    at = 0
    for ref in ins:
        width = ref.shape[1]
        shard_ref[:, at : at + width] = ref[...]
        at += width


def norm_back(value, gain, grad):
    inv = lax.rsqrt(jnp.mean(value * value, axis=-1, keepdims=True) + eps)
    scaled = grad * gain
    mean = jnp.mean(scaled * value, axis=-1, keepdims=True)
    back = scaled * inv - value * (inv * inv * inv * mean)
    return back, jnp.sum(grad * (value * inv), axis=0, keepdims=True)


def turn(value, cosine, sine):
    half = value.shape[-1] // 2
    first, second = value[:, :half], value[:, half:]
    return jnp.concatenate([first * cosine - second * sine, second * cosine + first * sine], 1)


def halves(side, value):
    if isinstance(value, tuple):
        mine, other = value
        first = jnp.where(side == 0, mine, other)
        return jnp.concatenate([first, jnp.where(side == 0, other, mine)], 1)
    half = value.shape[1] // 2
    first, second = value[:, :half], value[:, half:]
    return jnp.where(side == 0, first, second), jnp.where(side == 0, second, first)


def attend_kernel(
    heads,
    side_ref,
    x_ref,
    wm_ref,
    wo_ref,
    gq_ref,
    gk_ref,
    cos_ref,
    sin_ref,
    seg_row_ref,
    seg_col_ref,
    h1_ref,
    proj_ref,
    q_ref,
    k_ref,
    v_ref,
    p_ref,
    a_ref,
    o_ref,
    x2_ref,
    h2_ref,
    gains_ref,
):
    dim = k_ref.shape[1]
    wide_q = heads * dim
    wide_p = wide_q + 2 * dim
    length = x_ref.shape[0]
    source = x_ref[...].astype(F32)
    side = side_ref[0]
    gains = [jnp.transpose(w[:, wide_p : wide_p + 128].astype(F32))[:8] for w in (wm_ref, wo_ref)]
    gains = halves(side, tuple(gains))
    gains_ref[...] = gains
    h1 = rms_norm(source, gains[0:1])
    h1_ref[...] = h1.astype(BF16)
    h1m, h1o = halves(side, h1)
    proj = product(h1m.astype(BF16), wm_ref[:, :wide_p])
    proj = proj + product(h1o.astype(BF16), wo_ref[:, :wide_p])
    proj_ref[...] = proj[:, : wide_q + dim]
    value = proj[:, wide_q + dim :].astype(BF16)
    v_ref[...] = value
    cosine, sine = cos_ref[...], sin_ref[...]
    key = turn(rms_norm(proj[:, wide_q : wide_q + dim], gk_ref[...]), cosine, sine).astype(BF16)
    k_ref[...] = key
    row = lax.broadcasted_iota(jnp.int32, (length, length), 0)
    col = lax.broadcasted_iota(jnp.int32, (length, length), 1)
    allowed = (seg_col_ref[...] == seg_row_ref[...]) & (col <= row)
    for h in range(heads):
        cut = slice(h * dim, (h + 1) * dim)
        query = turn(rms_norm(proj[:, cut], gq_ref[...]), cosine, sine).astype(BF16)
        q_ref[:, cut] = query
        logits = jnp.where(allowed, against_cols(query, key) * dim ** (-0.5), -1e30)
        expo = jnp.exp(logits - jnp.max(logits, axis=-1, keepdims=True))
        probs = expo / jnp.sum(expo, axis=-1, keepdims=True)
        p_ref[h] = probs
        a_ref[:, cut] = product(probs.astype(BF16), value).astype(BF16)
    mixed = a_ref[...]
    out = [against_cols(mixed, w[:, wide_p + 128 :]) for w in (wm_ref, wo_ref)]
    out = halves(side, tuple(out))
    o_ref[...] = out
    middle = source + rms_norm(out, gains[1:2])
    x2_ref[...] = middle
    h2_ref[...] = rms_norm(middle, gains[2:3]).astype(BF16)


def added(own_ref, refs):
    value = own_ref[...]
    for ref in refs:
        value = value + ref[...].astype(F32)
    return value


def after_kernel(own_ref, *refs):
    x2_ref, c_ref, gains_ref, result_ref, df_ref, term_ref = refs[3:]
    value = added(own_ref, refs[:3])
    gain = gains_ref[3:4]
    result_ref[...] = (x2_ref[...] + rms_norm(value, gain)).astype(BF16)
    back, term = norm_back(value, gain, c_ref[...].astype(F32))
    df_ref[...] = back.astype(BF16)
    term_ref[...] = term


def attend_back_kernel(
    heads,
    side_ref,
    own_ref,
    *refs,
):
    got_refs, refs = refs[:3], refs[3:]
    (
    c_ref,
    x_ref,
    x2_ref,
    o_ref,
    gains_ref,
    ffn_out_ref,
    wm_ref,
    wo_ref,
    h1_ref,
    proj_ref,
    q_ref,
    k_ref,
    v_ref,
    p_ref,
    a_ref,
    gq_ref,
    gk_ref,
    cos_ref,
    sin_ref,
    grad_ref,
    mine_ref,
    other_ref,
    low_ref,
    ) = refs
    dim = k_ref.shape[1]
    wide_q = heads * dim
    wide_p = wide_q + 2 * dim
    side = side_ref[0]
    scale = dim ** (-0.5)
    gains = gains_ref[...]
    back, ffn_in_term = norm_back(x2_ref[...], gains[2:3], added(own_ref, got_refs))
    middle = c_ref[...].astype(F32) + back
    out_back, attn_out_term = norm_back(o_ref[...], gains[1:2], middle)
    out_low = [v.astype(BF16) for v in halves(side, out_back)]
    mixed = product(out_low[0], wm_ref[:, wide_p + 128 :])
    mixed = (mixed + product(out_low[1], wo_ref[:, wide_p + 128 :])).astype(BF16)
    key, value = k_ref[...], v_ref[...]
    cosine, sine = cos_ref[...], sin_ref[...]
    key_back, value_back, query_gain = 0.0, 0.0, 0.0
    for h in range(heads):
        cut = slice(h * dim, (h + 1) * dim)
        probs = p_ref[h]
        mixed_h = mixed[:, cut]
        probs_back = against_cols(mixed_h, value)
        value_back = value_back + across_rows(probs.astype(BF16), mixed_h)
        row_dot = jnp.sum(probs * probs_back, axis=-1, keepdims=True)
        score = (probs * (probs_back - row_dot) * scale).astype(BF16)
        key_back = key_back + across_rows(score, q_ref[:, cut])
        query_back = product(score, key).astype(BF16).astype(F32)
        query_back, term = norm_back(
            proj_ref[:, cut], gq_ref[...], turn(query_back, cosine, -sine)
        )
        query_gain = query_gain + term
        low_ref[:, cut] = query_back.astype(BF16)
    key_back = key_back.astype(BF16).astype(F32)
    key_back, key_gain = norm_back(
        proj_ref[:, wide_q : wide_q + dim], gk_ref[...], turn(key_back, cosine, -sine)
    )
    low_ref[:, wide_q : wide_q + dim] = key_back.astype(BF16)
    low_ref[:, wide_q + dim :] = value_back.astype(BF16)
    quarter = dim // 4
    small = [
        gain[:, i * quarter : (i + 1) * quarter]
        for gain in (query_gain, key_gain)
        for i in range(4)
    ]
    small = jnp.concatenate(small, 0)
    small = jnp.concatenate([jnp.zeros((8, 128 - quarter), F32), small], 1)
    low = low_ref[...]
    source = x_ref[...].astype(F32)
    back = [against_cols(low, w[:, :wide_p]) for w in (wm_ref, wo_ref)]
    back, attn_in_term = norm_back(source, gains[0:1], halves(side, tuple(back)))
    grad_ref[...] = (middle + back).astype(BF16)
    terms = jnp.concatenate([attn_in_term, attn_out_term, ffn_in_term, ffn_out_ref[...]], 0)
    terms = jnp.concatenate([terms, jnp.zeros((124, terms.shape[1]), F32)], 0)
    terms = halves(side, terms)
    h1 = halves(side, h1_ref[...].astype(F32))
    mixed_low = a_ref[...]
    for i, ref in enumerate((mine_ref, other_ref)):
        block = jnp.transpose(terms[i])
        ref[:, wide_p : wide_p + 128] = jnp.concatenate([block[:8] + small, block[8:]], 0).astype(BF16)
        ref[:, :wide_p] = across_rows(h1[i].astype(BF16), low).astype(BF16)
        ref[:, wide_p + 128 :] = across_rows(out_low[i], mixed_low).astype(BF16)


def chunks(width):
    return [slice(at, min(at + 256, width)) for at in range(0, width, 256)]


def ffn_kernel(count, *refs):
    block_refs, refs = refs[:count], refs[count:]
    gate_ref, up_ref, down_ref, x_ref, hid_ref, by_gate_ref, by_up_ref, *out_refs = refs
    rows = block_refs[0].shape[0]
    x = jnp.concatenate([ref[...] for ref in block_refs], 0)
    x_ref[...] = x
    root = (2.0 / 3.141592653589793) ** 0.5
    for cut in chunks(gate_ref.shape[1]):
        gate = product(x, gate_ref[:, cut])
        upper = product(x, up_ref[:, cut])
        square = gate * gate
        bent = jnp.tanh(root * gate * (1.0 + 0.044715 * square))
        half = 0.5 * (1.0 + bent)
        gelu = gate * half
        slope = half + 0.5 * gate * (1.0 - bent * bent) * root * (1.0 + 3 * 0.044715 * square)
        hid_ref[:, cut] = (gelu * upper).astype(BF16)
        by_gate_ref[:, cut] = (upper * slope).astype(BF16)
        by_up_ref[:, cut] = gelu.astype(BF16)
    out = against_cols(hid_ref[...], down_ref[...])
    for i, ref in enumerate(out_refs):
        ref[...] = out[i * rows : (i + 1) * rows].astype(ref.dtype)


def ffn_back_kernel(count, *refs):
    block_refs, refs = refs[:count], refs[count:]
    gate_ref, up_ref, down_ref, by_gate_ref, by_up_ref, df_ref, dgt_ref, dup_ref, *out_refs = refs
    rows = block_refs[0].shape[0]
    df = jnp.concatenate([ref[...] for ref in block_refs], 0)
    df_ref[...] = df
    for cut in chunks(gate_ref.shape[1]):
        grad = product(df, down_ref[:, cut])
        dgt_ref[:, cut] = (grad * by_gate_ref[:, cut].astype(F32)).astype(BF16)
        dup_ref[:, cut] = (grad * by_up_ref[:, cut].astype(F32)).astype(BF16)
    out = against_cols(dgt_ref[...], gate_ref[...]) + against_cols(dup_ref[...], up_ref[...])
    for i, ref in enumerate(out_refs):
        ref[...] = out[i * rows : (i + 1) * rows].astype(ref.dtype)


def ffn_grad_kernel(count, side_ref, *refs):
    def whole(kind):
        return jnp.concatenate([ref[...] for ref in refs[kind * count : (kind + 1) * count]], 0)

    mine_ref, other_ref = refs[5 * count :]
    side = side_ref[0]
    left = [[v.astype(BF16) for v in halves(side, whole(i).astype(F32))] for i in (0, 1)]
    for i, (pair, right) in enumerate(((0, 2), (1, 3), (1, 4))):
        right = whole(right)
        for half, ref in zip(left[pair], (mine_ref, other_ref)):
            ref[i] = across_rows(half, right).astype(BF16)


def call(kernel, outs, flops, scratch, *arrays, smem=0, room=40):
    size = 1 << 16
    spaces = [pltpu.SMEM] * smem + [None] * (len(arrays) - smem)
    return pl.pallas_call(
        kernel,
        out_shape=[jax.ShapeDtypeStruct(shape, kind) for shape, kind in outs],
        in_specs=[pl.BlockSpec(memory_space=space) for space in spaces],
        scratch_shapes=scratch,
        cost_estimate=pl.CostEstimate(flops=flops, bytes_accessed=size, transcendentals=0),
        compiler_params=pltpu.CompilerParams(vmem_limit_bytes=room << 20),
    )(*arrays)


def local(
    links,
    tokens,
    segment_ids,
    w_query,
    w_key,
    w_value,
    w_out,
    w_gate,
    w_up,
    w_down,
    g_attn_in,
    g_attn_out,
    g_ffn_in,
    g_ffn_out,
    g_query,
    g_key,
    cotangent,
):
    links.place()
    rows = w_query.shape[0]
    segments = segment_ids[0]
    head_dim = g_query.shape[0]
    wide_q = w_query.shape[1]
    wide_k = w_key.shape[1]
    wide_p = wide_q + 2 * wide_k
    wide_w = wide_p + 128 + wide_q
    heads = wide_q // head_dim
    length, width = tokens.shape[1:]
    most = ffn_cut(w_gate.shape[1])[1]
    seat = links.lo[None].astype(jnp.int32)
    source, upstream = tokens[0], cotangent[0]

    gains = jnp.pad(jnp.stack([g_attn_in, g_attn_out, g_ffn_in, g_ffn_out], 1), ((0, 0), (0, 124)))
    (shard,) = call(
        pack_kernel,
        [((rows, wide_w), BF16)],
        1 << 20,
        [],
        w_query,
        w_key,
        w_value,
        gains,
        jnp.transpose(w_out),
        room=62,
    )
    packed = call(
        ffn_pack_kernel,
        [((3, rows, most), BF16)] * TEAM,
        1 << 20,
        [],
        seat,
        w_gate,
        w_up,
        jnp.transpose(w_down),
        smem=1,
        room=62,
    )
    places = links.blocks((0, 3, 4, 7, 1, 2, 5, 6))
    places_back = links.blocks((6, 7, 4, 5, 0, 1, 2, 3))
    count = len(places)
    fetch = Stream((packed[how[0] % TEAM], how) for how, _ in places)
    teams = range(links.half)
    _, crossed = point(links, [], [(shard, links.cross(t)) for t in teams])
    fetch.sends.append((lambda: jnp.stack(fetch.got[:count]), None))
    got = {}
    for some in spread(
        links,
        jnp.stack(crossed) if links.half > 1 else crossed[0][None],
        ([(fetch, 0, 2)], [(fetch, 2, 2)], [(fetch, 2, 2)]),
    ):
        got.update(some)
    mine = jnp.zeros((count, rows, wide_w), BF16)
    for number in range(TEAM):
        for t in teams:
            at = ((links.hi ^ t) % links.half) * TEAM + links.seat(number)
            mine = lax.dynamic_update_slice_in_dim(mine, got[number][t : t + 1], at, 0)
    mine = mine.reshape(count * rows, wide_w)
    (mine,), (other,) = point(links, [mine], [(mine, None)], (fetch, 2, count - 6))
    weights = (mine, other)
    side = links.mine[None].astype(jnp.int32)

    cosine, sine = rope_tables(positions(segments), head_dim)
    gain_q = g_query.astype(F32)[None]
    gain_k = g_key.astype(F32)[None]
    normed, proj, query, key, value, probs, mixed, out, middle, normed_two, gains = call(
        functools.partial(attend_kernel, heads),
        [
            ((length, width), BF16),
            ((length, wide_q + wide_k), F32),
            ((length, wide_q), BF16),
            ((length, wide_k), BF16),
            ((length, wide_k), BF16),
            ((heads, length, length), F32),
            ((length, wide_q), BF16),
            ((length, width), F32),
            ((length, width), F32),
            ((length, width), BF16),
            ((8, width), F32),
        ],
        4 * length * mine.size,
        [],
        side,
        source,
        *weights,
        gain_q,
        gain_k,
        cosine,
        sine,
        segments[None],
        segments[:, None],
        smem=1,
        room=62,
    )

    def put(half, blocks):
        def made(arrays):
            for n, (_, place) in enumerate(places):
                block = blocks()[n]
                arrays = [
                    lax.dynamic_update_slice_in_dim(w, block[i : i + 1], half * count + place, 0)
                    for i, w in enumerate(arrays)
                ]
            return arrays

        return made

    held = Held(
        [jnp.zeros((links.nf, rows, most), BF16) for _ in range(3)],
        [
            lambda arrays: arrays,
            put(links.mine, lambda: fetch.got),
            put(links.other, lambda: fetch.got[count]),
        ],
    )
    plans = ([(fetch, count - 6, 1)], [(fetch, 1, 0)], [])
    team_in = list(spread(links, normed_two, plans, held))
    early = count - 2
    ffn_w = held.arrays
    ffn_w = [w.reshape(links.nf * rows, most) for w in ffn_w]

    def wave(kernel, blocks, *more):
        size = len(blocks) * length
        kept = [((size, width), BF16)] + [((size, most), BF16)] * (3 if not more else 2)
        out = call(
            functools.partial(kernel, len(blocks)),
            kept + [((length, width), F32 if n == 0 else BF16) for n in blocks],
            1 << 20,
            [],
            *blocks.values(),
            *ffn_w,
            *more,
        )
        return out[: len(kept)], dict(zip(blocks, out[len(kept) :]))

    def share(steps, kernel, extra=((),) * 3):
        kept, part = [], {}
        for blocks, more in zip(steps, extra):
            keep, terms = wave(kernel, blocks, *more)
            kept.append(keep)
            part.update(terms)
        return kept, part

    kept, part = share(team_in, ffn_kernel)
    [(own, *got)] = collect(links, [part], ((), (), ()))
    result, ffn_proj_grad, ffn_out_term = call(
        after_kernel,
        [((length, width), BF16), ((length, width), BF16), ((1, width), F32)],
        1 << 20,
        [],
        own,
        *got,
        middle,
        upstream,
        gains,
    )
    kept_back, part = share(
        spread(links, ffn_proj_grad), ffn_back_kernel, [keep[2:] for keep in kept]
    )
    kinds = [
        [k[0] for k in kept_back],
        [k[0] for k in kept],
        [k[1] for k in kept],
        [k[1] for k in kept_back],
        [k[2] for k in kept_back],
    ]

    made = []

    def grads(sends):
        arrays, values = lax.optimization_barrier(
            ([v for kind in kinds for v in kind], [v for v, _ in sends])
        )
        made.extend(
            call(
                functools.partial(ffn_grad_kernel, len(kept)),
                [((3, width // 2, most), BF16)] * 2,
                1 << 20,
                [],
                side,
                *arrays,
                smem=1,
            )
        )
        mine, other = made
        _, (swapped,) = point(links, [], [(other, None)])

        def block(place):
            both = [lax.dynamic_slice_in_dim(v, place * rows, rows, 1) for v in (mine, swapped)]
            return (both[0].astype(F32) + both[1].astype(F32)).astype(BF16)

        back.sends = [
            (functools.partial(block, place), how) for how, place in places_back
        ]
        back.sends.append((lambda: jnp.stack(back.got[:early]), None))
        return [(v, how) for v, (_, how) in zip(values, sends)]

    back = Stream([])
    [(own, *got)] = collect(links, [part], ((), (), ()), hook=grads)
    (own, *got), _ = point(links, [own] + got, [], (back, 0, 1))

    source_grad, mine, other = call(
        functools.partial(attend_back_kernel, heads),
        [
            ((length, width), BF16),
            ((width // 2, wide_w), BF16),
            ((width // 2, wide_w), BF16),
        ],
        1 << 20,
        [pltpu.VMEM((length, wide_p), BF16)],
        side,
        own,
        *got,
        upstream,
        source,
        middle,
        out,
        gains,
        ffn_out_term,
        *weights,
        normed,
        proj,
        query,
        key,
        value,
        probs,
        mixed,
        gain_q,
        gain_k,
        cosine,
        sine,
        smem=1,
    )
    (mine,), (got,) = point(links, [mine], [(other, None)], (back, 1, 2))
    quarter = head_dim // 4
    col = wide_p + 128 - quarter
    small = mine[:8, col : col + quarter]
    sums = Sum(small, col)
    sums.add(got)

    def owned(t, number):
        at = (((links.hi ^ t) % links.half) * TEAM + links.seat(number)) * rows
        first, second = (lax.dynamic_slice_in_dim(v, at, rows, 0) for v in (mine, got))
        return first.astype(F32) + second.astype(F32)

    parts = [{number: owned(t, number) for number in range(TEAM)} for t in teams]
    plans = ([(back, 1, 1)], [(back, 1, 2)], [(back, 2, 1)])
    done = collect(links, parts, plans, sums)
    done = [sum(v.astype(F32) for v in d) for d in done]
    done = [d.astype(BF16) for d in done]
    done[0] = sums.put(done[0])
    sends = [(d, links.cross(t)) for t, d in zip(teams, done)]
    _, got = point(links, [], sends, (back, 2, 1))
    sums.add(got[0])
    total = sums.put(sum(g.astype(F32) for g in got).astype(BF16))
    (total,), (other,) = point(links, [total], [(total, None)], (back, 1, count))
    shard = total.astype(F32) + other.astype(F32)
    both = jnp.where(links.r == 1, total[:8, col : col + quarter], other[:8, col : col + quarter])
    if links.half > 1:
        both = everywhere(links, small)
    gain_sums = both.astype(F32).reshape(2, head_dim)
    gain_shard = shard[:, wide_p : wide_p + 128]
    point(links, [], [], (back, count + 1, 0))
    other_first = back.got.pop(count)
    _, (other_last,) = point(links, [], [(jnp.stack(back.got[early:]), None)])
    order = [how[0] % TEAM for how, _ in places_back[:TEAM]]
    ffn_grads = None
    for t in teams:
        own = back.got[t * TEAM : (t + 1) * TEAM]
        if links.half == 1:
            others = [other_first, other_last]
        else:
            others = [jnp.concatenate([other_first, other_last])[t * TEAM : (t + 1) * TEAM]]
        if rows % 8:
            others = [some[n] for some in others for n in range(some.shape[0])]
            done = jnp.zeros((3,) + w_gate.shape, F32)
            for k, block, other in zip(order, own, others):
                at, _, _ = ffn_window(links.lo ^ k, w_gate.shape[1])
                block = block.astype(F32) + other.astype(F32)
                block = block + lax.dynamic_slice_in_dim(done, at, most, 2)
                done = lax.dynamic_update_slice_in_dim(done, block, at, 2)
            ffn_grads = done if ffn_grads is None else ffn_grads + done
            continue
        done = call(
            functools.partial(ffn_unpack_kernel, order),
            [(w_gate.shape, F32)] * 3,
            1 << 20,
            [],
            seat,
            *own,
            *others,
            smem=1,
            room=62,
        )
        ffn_grads = done if ffn_grads is None else [a + b for a, b in zip(ffn_grads, done)]
    down_grad, gate_grad, up_grad = ffn_grads
    return (
        result[None],
        source_grad[None],
        shard[:, :wide_q],
        shard[:, wide_q : wide_q + wide_k],
        shard[:, wide_q + wide_k : wide_p],
        jnp.transpose(shard[:, wide_p + 128 :]),
        gate_grad,
        up_grad,
        jnp.transpose(down_grad),
        gain_shard[:, 0],
        gain_shard[:, 1],
        gain_shard[:, 2],
        gain_shard[:, 3],
        gain_sums[0],
        gain_sums[1],
    )


def solution(mesh):
    links = Links(mesh)
    rows = P(("fsdp", "rep"), None, None)
    placed = (
        rows,
        P(("fsdp", "rep"), None),
        P("fsdp", None),
        P("fsdp", None),
        P("fsdp", None),
        P(None, "fsdp"),
        P("fsdp", None),
        P("fsdp", None),
        P(None, "fsdp"),
        P("fsdp"),
        P("fsdp"),
        P("fsdp"),
        P("fsdp"),
        P(),
        P(),
        rows,
    )
    return jax.shard_map(
        lambda *arrays: local(links, *arrays),
        mesh=mesh,
        in_specs=placed,
        out_specs=(rows, rows) + placed[2:13] + (P(), P()),
        check_vma=False,
    )
```

```python
import functools

import jax
import jax.numpy as jnp
from jax import lax
from jax.experimental import pallas as pl
from jax.experimental.pallas import tpu as pltpu
from jax.sharding import PartitionSpec as P

eps = 1e-06


def rms_norm(value, gain):
    return value * lax.rsqrt(jnp.mean(value * value, axis=-1, keepdims=True) + eps) * gain


def positions(segments):
    earlier = (segments[None, :] < segments[:, None]).astype(jnp.int32)
    return jnp.arange(segments.shape[0], dtype=jnp.int32) - jnp.sum(earlier, axis=1)


def rope_tables(where, width):
    half = width // 2
    expo = jnp.arange(half, dtype=jnp.float32) * (2.0 / width)
    freq = jnp.exp(-expo * jnp.log(1000000.0))
    angle = where.astype(jnp.float32)[:, None] * freq[None, :]
    return (jnp.cos(angle), jnp.sin(angle))


def rotate(value, cosine, sine):
    half = value.shape[-1] // 2
    first = value[..., :half]
    second = value[..., half:]
    cosine = cosine[:, None, :]
    sine = sine[:, None, :]
    return jnp.concatenate(
        [first * cosine - second * sine, second * cosine + first * sine], axis=-1
    )


def geglu(gate, upper):
    return jax.nn.gelu(gate, approximate=True) * upper


def across_rows(left, right):
    return lax.dot_general(
        left, right, (((0,), (0,)), ((), ())), preferred_element_type=jnp.float32
    )


def against_cols(left, right):
    return lax.dot_general(
        left, right, (((1,), (1,)), ((), ())), preferred_element_type=jnp.float32
    )


def product(left, right):
    return jnp.dot(left, right, preferred_element_type=jnp.float32)


TEAM = 8
BF16 = jnp.bfloat16
F32 = jnp.float32


class Links:
    def __init__(self, mesh):
        self.nf = mesh.shape["fsdp"]
        self.nr = mesh.shape["rep"]
        assert self.nr == 2 and self.nf % (2 * TEAM) == 0 and self.nf & (self.nf - 1) == 0
        self.teams = self.nf // TEAM
        self.half = self.teams // 2

    def place(self):
        self.f = lax.axis_index("fsdp")
        self.r = lax.axis_index("rep")
        self.lo = self.f % TEAM
        self.hi = self.f // TEAM
        side = self.hi // self.half
        self.mine = side ^ self.r
        self.other = side ^ (1 - self.r)

    def seat(self, number):
        first, second = role(number)
        return self.lo ^ jnp.where(self.r == 0, first, second)

    def go(self, value, how):
        if how is None:
            return lax.ppermute(value, "rep", [(0, 1), (1, 0)])
        pairs = [
            (f * self.nr + r, (f ^ how[r]) * self.nr + r)
            for f in range(self.nf)
            for r in range(self.nr)
            if how[r] is not None
        ]
        return lax.ppermute(value, ("fsdp", "rep"), pairs)

    def both(self, offset):
        return offset, offset

    def cross(self, team):
        return team * TEAM, (self.half + team) * TEAM

    def half_rows(self, value, side, axis=0):
        size = value.shape[axis] // 2
        return lax.dynamic_slice_in_dim(value, side * size, size, axis)

    def blocks(self, order):
        return [
            (
                (t * TEAM + k, (self.half + t) * TEAM + k),
                ((self.hi ^ t) % self.half) * TEAM + (self.lo ^ k),
            )
            for t in range(self.half)
            for k in order
        ]


ROLE_BITS = ((1, 2, 4), (2, 4, 1))


def role(number):
    return tuple(
        sum(bits[i] for i in range(3) if number >> i & 1) for bits in ROLE_BITS
    )


class Stream:
    def __init__(self, sends):
        self.sends = list(sends)
        self.got = []
        self.seen = 0

    def oldest(self, count):
        return self.got[self.seen : self.seen + count]

    def waited(self, values):
        self.got[self.seen : self.seen + len(values)] = values
        self.seen += len(values)

    def next(self, count):
        out, self.sends = self.sends[:count], self.sends[count:]
        return [(value() if callable(value) else value, how) for value, how in out]

    def sent(self, values):
        self.got += values


class Held:
    def __init__(self, arrays, steps):
        self.arrays = arrays
        self.steps = steps

    def before(self, n):
        self.arrays = self.steps[n](self.arrays)
        return self.arrays


def everywhere(links, value):
    value = value.astype(F32)
    value = value + links.go(value, None)
    for bit in range(links.nf.bit_length() - 1):
        value = value + links.go(value, links.both(1 << bit))
    return value


def point(links, waits, sends, *streams):
    olds = [stream.oldest(w) for stream, w, _ in streams]
    waits, olds, values = lax.optimization_barrier((waits, olds, [v for v, _ in sends]))
    for (stream, _, _), old in zip(streams, olds):
        stream.waited(old)
    mores = [stream.next(s) for stream, _, s in streams]
    flat = [v for more in mores for v, _ in more]
    waits, olds, values, flat = lax.optimization_barrier((waits, olds, values, flat))
    for (stream, _, _), old in zip(streams, olds):
        stream.got[stream.seen - len(old) : stream.seen] = old
    got = [links.go(v, how) for v, (_, how) in zip(values, sends)]
    flat = iter(flat)
    for (stream, _, _), more in zip(streams, mores):
        stream.sent([links.go(next(flat), how) for _, how in more])
    return waits, got


def spread(links, value, plans=((), (), ()), held=None):
    by = {n: role(n) for n in (1, 2, 4)}

    def step(n, waits, sends):
        (waits, made), got = point(links, [waits, held.before(n) if held else []], sends, *plans[n])
        if held:
            held.arrays = made
        return waits, got

    _, (one, two, four) = step(0, [], [(value, by[n]) for n in (1, 2, 4)])
    yield {0: value, 1: one, 2: two, 4: four}
    sends = [(one, by[2]), (four, by[1]), (two, by[4])]
    near, (three, five, six) = step(1, [one, two, four], sends)
    far, (seven,) = step(2, [three, five], [(six, by[1])])
    yield {3: far[0], 5: far[1], 6: six}
    yield {7: seven}


class Sum:
    def __init__(self, value, col):
        self.value = value
        self.col = col

    def put(self, block):
        rows, cols = self.value.shape
        row = lax.broadcasted_iota(jnp.int32, block.shape, 0)
        col = lax.broadcasted_iota(jnp.int32, block.shape, 1)
        own = (row < rows) & (col >= self.col) & (col < self.col + cols)
        edges = ((0, block.shape[0] - rows), (self.col, block.shape[1] - self.col - cols))
        return jnp.where(own, jnp.pad(self.value, edges), block)

    def add(self, block):
        rows, cols = self.value.shape
        other = block[:rows, self.col : self.col + cols]
        self.value = (self.value.astype(F32) + other.astype(F32)).astype(BF16)


def collect(links, parts, plans, extra=None, hook=None):
    by = {n: role(n) for n in (1, 2, 4)}

    def add(part, number, block):
        return part[number].astype(F32) + block.astype(F32)

    def carry(blocks):
        return [extra.put(b) if extra and i == 0 else b for i, b in enumerate(blocks)]

    def carried(blocks):
        if extra:
            extra.add(blocks[0])

    sends = carry([p[7].astype(BF16) for p in parts])
    _, got = point(links, [], [(v, by[1]) for v in sends], *plans[0])
    carried(got)
    sixes = carry([add(p, 6, v).astype(BF16) for p, v in zip(parts, got)])
    sends = []
    for part, six in zip(parts, sixes):
        sends += [(six, by[4]), (part[5].astype(BF16), by[1]), (part[3].astype(BF16), by[2])]
    if hook:
        sends = hook(sends)
    _, got = point(links, [], sends, *plans[1])
    carried(got)
    twos = carry([add(p, 2, got[3 * i]).astype(BF16) for i, p in enumerate(parts)])
    sends = []
    for i, (part, two) in enumerate(zip(parts, twos)):
        sends.append((two, by[2]))
        for n, j in ((4, 1), (1, 2)):
            sends.append((add(part, n, got[3 * i + j]).astype(BF16), by[n]))
    _, got = point(links, [], sends, *plans[2])
    carried(got)
    return [(p[0], *got[3 * i : 3 * i + 3]) for i, p in enumerate(parts)]


def ffn_cut(width):
    tiles = width // 128
    most = -(-tiles // TEAM)
    return TEAM - (most * TEAM - tiles), most * 128


def ffn_window(seat, width):
    full, most = ffn_cut(width)
    start = seat * most - jnp.maximum(seat - full, 0) * 128
    at = jnp.minimum(start, width - most)
    size = jnp.where(seat < full, most, most - 128)
    return at, start - at, start - at + size


def ffn_pack_kernel(seat_ref, gate_ref, up_ref, down_ref, *out_refs):
    width = gate_ref.shape[1]
    rows, most = out_refs[0].shape[1:]
    col = lax.broadcasted_iota(jnp.int32, (rows, most), 1)
    for k in range(TEAM):
        at, first, end = ffn_window(seat_ref[0] ^ k, width)
        own = (col >= first) & (col < end)
        for i, ref in enumerate((gate_ref, up_ref, down_ref)):
            block = ref[:, pl.ds(pl.multiple_of(at, 128), most)].astype(F32)
            out_refs[k][i] = jnp.where(own, block, 0.0).astype(BF16)


def ffn_unpack_kernel(order, seat_ref, *refs):
    block_refs, other_refs, out_refs = refs[:TEAM], refs[TEAM:-3], refs[-3:]
    width = out_refs[0].shape[1]
    most = block_refs[0].shape[2]
    others = [ref.at[n] for ref in other_refs for n in range(ref.shape[0])]
    less = most - 128

    def place(k, block, other):
        at, first, end = ffn_window(seat_ref[0] ^ k, width)
        start = pl.multiple_of(at + first, 128)
        for skip, size in ((0, most), (0, less), (128, less)):

            @pl.when((end - first == size) & (first == skip))
            def _(skip=skip, size=size):
                cut = slice(skip, skip + size)
                for i, out_ref in enumerate(out_refs):
                    value = block[i, :, cut].astype(F32) + other[i, :, cut].astype(F32)
                    out_ref[:, pl.ds(start, size)] = value

    for k, block, other in zip(order, block_refs, others):
        place(k, block, other)


def pack_kernel(*refs):
    ins, shard_ref = refs[:-1], refs[-1]
    at = 0
    for ref in ins:
        width = ref.shape[1]
        shard_ref[:, at : at + width] = ref[...]
        at += width


def norm_back(value, gain, grad):
    inv = lax.rsqrt(jnp.mean(value * value, axis=-1, keepdims=True) + eps)
    scaled = grad * gain
    mean = jnp.mean(scaled * value, axis=-1, keepdims=True)
    back = scaled * inv - value * (inv * inv * inv * mean)
    return back, jnp.sum(grad * (value * inv), axis=0, keepdims=True)


def turn(value, cosine, sine):
    half = value.shape[-1] // 2
    first, second = value[:, :half], value[:, half:]
    return jnp.concatenate([first * cosine - second * sine, second * cosine + first * sine], 1)


def halves(side, value):
    if isinstance(value, tuple):
        mine, other = value
        first = jnp.where(side == 0, mine, other)
        return jnp.concatenate([first, jnp.where(side == 0, other, mine)], 1)
    half = value.shape[1] // 2
    first, second = value[:, :half], value[:, half:]
    return jnp.where(side == 0, first, second), jnp.where(side == 0, second, first)


def attend_kernel(
    heads,
    side_ref,
    x_ref,
    wm_ref,
    wo_ref,
    gq_ref,
    gk_ref,
    cos_ref,
    sin_ref,
    seg_row_ref,
    seg_col_ref,
    h1_ref,
    proj_ref,
    q_ref,
    k_ref,
    v_ref,
    p_ref,
    a_ref,
    o_ref,
    x2_ref,
    h2_ref,
    gains_ref,
):
    dim = k_ref.shape[1]
    wide_q = heads * dim
    wide_p = wide_q + 2 * dim
    length = x_ref.shape[0]
    source = x_ref[...].astype(F32)
    side = side_ref[0]
    gains = [jnp.transpose(w[:, wide_p : wide_p + 128].astype(F32))[:8] for w in (wm_ref, wo_ref)]
    gains = halves(side, tuple(gains))
    gains_ref[...] = gains
    h1 = rms_norm(source, gains[0:1])
    h1_ref[...] = h1.astype(BF16)
    h1m, h1o = halves(side, h1)
    proj = product(h1m.astype(BF16), wm_ref[:, :wide_p])
    proj = proj + product(h1o.astype(BF16), wo_ref[:, :wide_p])
    proj_ref[...] = proj[:, : wide_q + dim]
    value = proj[:, wide_q + dim :].astype(BF16)
    v_ref[...] = value
    cosine, sine = cos_ref[...], sin_ref[...]
    key = turn(rms_norm(proj[:, wide_q : wide_q + dim], gk_ref[...]), cosine, sine).astype(BF16)
    k_ref[...] = key
    row = lax.broadcasted_iota(jnp.int32, (length, length), 0)
    col = lax.broadcasted_iota(jnp.int32, (length, length), 1)
    allowed = (seg_col_ref[...] == seg_row_ref[...]) & (col <= row)
    for h in range(heads):
        cut = slice(h * dim, (h + 1) * dim)
        query = turn(rms_norm(proj[:, cut], gq_ref[...]), cosine, sine).astype(BF16)
        q_ref[:, cut] = query
        logits = jnp.where(allowed, against_cols(query, key) * dim ** (-0.5), -1e30)
        expo = jnp.exp(logits - jnp.max(logits, axis=-1, keepdims=True))
        probs = expo / jnp.sum(expo, axis=-1, keepdims=True)
        p_ref[h] = probs
        a_ref[:, cut] = product(probs.astype(BF16), value).astype(BF16)
    mixed = a_ref[...]
    out = [against_cols(mixed, w[:, wide_p + 128 :]) for w in (wm_ref, wo_ref)]
    out = halves(side, tuple(out))
    o_ref[...] = out
    middle = source + rms_norm(out, gains[1:2])
    x2_ref[...] = middle
    h2_ref[...] = rms_norm(middle, gains[2:3]).astype(BF16)


def added(own_ref, refs):
    value = own_ref[...]
    for ref in refs:
        value = value + ref[...].astype(F32)
    return value


def after_kernel(own_ref, *refs):
    x2_ref, c_ref, gains_ref, result_ref, df_ref, term_ref = refs[3:]
    value = added(own_ref, refs[:3])
    gain = gains_ref[3:4]
    result_ref[...] = (x2_ref[...] + rms_norm(value, gain)).astype(BF16)
    back, term = norm_back(value, gain, c_ref[...].astype(F32))
    df_ref[...] = back.astype(BF16)
    term_ref[...] = term


def attend_back_kernel(
    heads,
    side_ref,
    own_ref,
    *refs,
):
    got_refs, refs = refs[:3], refs[3:]
    (
    c_ref,
    x_ref,
    x2_ref,
    o_ref,
    gains_ref,
    ffn_out_ref,
    wm_ref,
    wo_ref,
    h1_ref,
    proj_ref,
    q_ref,
    k_ref,
    v_ref,
    p_ref,
    a_ref,
    gq_ref,
    gk_ref,
    cos_ref,
    sin_ref,
    grad_ref,
    mine_ref,
    other_ref,
    low_ref,
    ) = refs
    dim = k_ref.shape[1]
    wide_q = heads * dim
    wide_p = wide_q + 2 * dim
    side = side_ref[0]
    scale = dim ** (-0.5)
    gains = gains_ref[...]
    back, ffn_in_term = norm_back(x2_ref[...], gains[2:3], added(own_ref, got_refs))
    middle = c_ref[...].astype(F32) + back
    out_back, attn_out_term = norm_back(o_ref[...], gains[1:2], middle)
    out_low = [v.astype(BF16) for v in halves(side, out_back)]
    mixed = product(out_low[0], wm_ref[:, wide_p + 128 :])
    mixed = (mixed + product(out_low[1], wo_ref[:, wide_p + 128 :])).astype(BF16)
    key, value = k_ref[...], v_ref[...]
    cosine, sine = cos_ref[...], sin_ref[...]
    key_back, value_back, query_gain = 0.0, 0.0, 0.0
    for h in range(heads):
        cut = slice(h * dim, (h + 1) * dim)
        probs = p_ref[h]
        mixed_h = mixed[:, cut]
        probs_back = against_cols(mixed_h, value)
        value_back = value_back + across_rows(probs.astype(BF16), mixed_h)
        row_dot = jnp.sum(probs * probs_back, axis=-1, keepdims=True)
        score = (probs * (probs_back - row_dot) * scale).astype(BF16)
        key_back = key_back + across_rows(score, q_ref[:, cut])
        query_back = product(score, key).astype(BF16).astype(F32)
        query_back, term = norm_back(
            proj_ref[:, cut], gq_ref[...], turn(query_back, cosine, -sine)
        )
        query_gain = query_gain + term
        low_ref[:, cut] = query_back.astype(BF16)
    key_back = key_back.astype(BF16).astype(F32)
    key_back, key_gain = norm_back(
        proj_ref[:, wide_q : wide_q + dim], gk_ref[...], turn(key_back, cosine, -sine)
    )
    low_ref[:, wide_q : wide_q + dim] = key_back.astype(BF16)
    low_ref[:, wide_q + dim :] = value_back.astype(BF16)
    quarter = dim // 4
    small = [
        gain[:, i * quarter : (i + 1) * quarter]
        for gain in (query_gain, key_gain)
        for i in range(4)
    ]
    small = jnp.concatenate(small, 0)
    small = jnp.concatenate([jnp.zeros((8, 128 - quarter), F32), small], 1)
    low = low_ref[...]
    source = x_ref[...].astype(F32)
    back = [against_cols(low, w[:, :wide_p]) for w in (wm_ref, wo_ref)]
    back, attn_in_term = norm_back(source, gains[0:1], halves(side, tuple(back)))
    grad_ref[...] = (middle + back).astype(BF16)
    terms = jnp.concatenate([attn_in_term, attn_out_term, ffn_in_term, ffn_out_ref[...]], 0)
    terms = jnp.concatenate([terms, jnp.zeros((124, terms.shape[1]), F32)], 0)
    terms = halves(side, terms)
    h1 = halves(side, h1_ref[...].astype(F32))
    mixed_low = a_ref[...]
    for i, ref in enumerate((mine_ref, other_ref)):
        block = jnp.transpose(terms[i])
        ref[:, wide_p : wide_p + 128] = jnp.concatenate([block[:8] + small, block[8:]], 0).astype(BF16)
        ref[:, :wide_p] = across_rows(h1[i].astype(BF16), low).astype(BF16)
        ref[:, wide_p + 128 :] = across_rows(out_low[i], mixed_low).astype(BF16)


def chunks(width):
    return [slice(at, min(at + 256, width)) for at in range(0, width, 256)]


def ffn_kernel(count, *refs):
    block_refs, refs = refs[:count], refs[count:]
    gate_ref, up_ref, down_ref, x_ref, hid_ref, by_gate_ref, by_up_ref, *out_refs = refs
    rows = block_refs[0].shape[0]
    x = jnp.concatenate([ref[...] for ref in block_refs], 0)
    x_ref[...] = x
    root = (2.0 / 3.141592653589793) ** 0.5
    for cut in chunks(gate_ref.shape[1]):
        gate = product(x, gate_ref[:, cut])
        upper = product(x, up_ref[:, cut])
        square = gate * gate
        bent = jnp.tanh(root * gate * (1.0 + 0.044715 * square))
        half = 0.5 * (1.0 + bent)
        gelu = gate * half
        slope = half + 0.5 * gate * (1.0 - bent * bent) * root * (1.0 + 3 * 0.044715 * square)
        hid_ref[:, cut] = (gelu * upper).astype(BF16)
        by_gate_ref[:, cut] = (upper * slope).astype(BF16)
        by_up_ref[:, cut] = gelu.astype(BF16)
    out = against_cols(hid_ref[...], down_ref[...])
    for i, ref in enumerate(out_refs):
        ref[...] = out[i * rows : (i + 1) * rows].astype(ref.dtype)


def ffn_back_kernel(count, *refs):
    block_refs, refs = refs[:count], refs[count:]
    gate_ref, up_ref, down_ref, by_gate_ref, by_up_ref, df_ref, dgt_ref, dup_ref, *out_refs = refs
    rows = block_refs[0].shape[0]
    df = jnp.concatenate([ref[...] for ref in block_refs], 0)
    df_ref[...] = df
    for cut in chunks(gate_ref.shape[1]):
        grad = product(df, down_ref[:, cut])
        dgt_ref[:, cut] = (grad * by_gate_ref[:, cut].astype(F32)).astype(BF16)
        dup_ref[:, cut] = (grad * by_up_ref[:, cut].astype(F32)).astype(BF16)
    out = against_cols(dgt_ref[...], gate_ref[...]) + against_cols(dup_ref[...], up_ref[...])
    for i, ref in enumerate(out_refs):
        ref[...] = out[i * rows : (i + 1) * rows].astype(ref.dtype)


def ffn_grad_kernel(count, side_ref, *refs):
    def whole(kind):
        return jnp.concatenate([ref[...] for ref in refs[kind * count : (kind + 1) * count]], 0)

    mine_ref, other_ref = refs[5 * count :]
    half = mine_ref.shape[1]
    left = [whole(0), whole(1)]
    for i, (pair, right) in enumerate(((0, 2), (1, 3), (1, 4))):
        term = across_rows(left[pair], whole(right)).astype(BF16)
        for side, refs_here in enumerate(((mine_ref, other_ref), (other_ref, mine_ref))):

            @pl.when(side_ref[0] == side)
            def _(i=i, term=term, refs_here=refs_here):
                refs_here[0][i] = term[:half]
                refs_here[1][i] = term[half:]


def call(kernel, outs, flops, scratch, *arrays, smem=0, room=24):
    size = 1 << 16
    spaces = [pltpu.SMEM] * smem + [None] * (len(arrays) - smem)
    return pl.pallas_call(
        kernel,
        out_shape=[jax.ShapeDtypeStruct(shape, kind) for shape, kind in outs],
        in_specs=[pl.BlockSpec(memory_space=space) for space in spaces],
        scratch_shapes=scratch,
        cost_estimate=pl.CostEstimate(flops=flops, bytes_accessed=size, transcendentals=0),
        compiler_params=pltpu.CompilerParams(vmem_limit_bytes=room << 20),
    )(*arrays)


def local(
    links,
    tokens,
    segment_ids,
    w_query,
    w_key,
    w_value,
    w_out,
    w_gate,
    w_up,
    w_down,
    g_attn_in,
    g_attn_out,
    g_ffn_in,
    g_ffn_out,
    g_query,
    g_key,
    cotangent,
):
    links.place()
    rows = w_query.shape[0]
    segments = segment_ids[0]
    head_dim = g_query.shape[0]
    wide_q = w_query.shape[1]
    wide_k = w_key.shape[1]
    wide_p = wide_q + 2 * wide_k
    wide_w = wide_p + 128 + wide_q
    heads = wide_q // head_dim
    length, width = tokens.shape[1:]
    most = ffn_cut(w_gate.shape[1])[1]
    seat = links.lo[None].astype(jnp.int32)
    source, upstream = tokens[0], cotangent[0]

    gains = jnp.pad(jnp.stack([g_attn_in, g_attn_out, g_ffn_in, g_ffn_out], 1), ((0, 0), (0, 124)))
    (shard,) = call(
        pack_kernel,
        [((rows, wide_w), BF16)],
        1 << 20,
        [],
        w_query,
        w_key,
        w_value,
        gains,
        jnp.transpose(w_out),
        room=62,
    )
    packed = call(
        ffn_pack_kernel,
        [((3, rows, most), BF16)] * TEAM,
        1 << 20,
        [],
        seat,
        w_gate,
        w_up,
        jnp.transpose(w_down),
        smem=1,
        room=62,
    )
    places = links.blocks((0, 3, 4, 7, 1, 2, 5, 6))
    places_back = links.blocks((6, 7, 4, 5, 0, 1, 2, 3))
    count = len(places)
    fetch = Stream((packed[how[0] % TEAM], how) for how, _ in places)
    teams = range(links.half)
    _, crossed = point(links, [], [(shard, links.cross(t)) for t in teams])
    fetch.sends.append((lambda: jnp.stack(fetch.got[:count]), None))
    got = {}
    for some in spread(
        links,
        jnp.stack(crossed) if links.half > 1 else crossed[0][None],
        ([(fetch, 0, 2)], [(fetch, 2, 2)], [(fetch, 2, 2)]),
    ):
        got.update(some)
    mine = jnp.zeros((count, rows, wide_w), BF16)
    for number in range(TEAM):
        for t in teams:
            at = ((links.hi ^ t) % links.half) * TEAM + links.seat(number)
            mine = lax.dynamic_update_slice_in_dim(mine, got[number][t : t + 1], at, 0)
    mine = mine.reshape(count * rows, wide_w)
    (mine,), (other,) = point(links, [mine], [(mine, None)], (fetch, 2, count - 6))
    weights = (mine, other)
    side = links.mine[None].astype(jnp.int32)

    cosine, sine = rope_tables(positions(segments), head_dim)
    gain_q = g_query.astype(F32)[None]
    gain_k = g_key.astype(F32)[None]
    normed, proj, query, key, value, probs, mixed, out, middle, normed_two, gains = call(
        functools.partial(attend_kernel, heads),
        [
            ((length, width), BF16),
            ((length, wide_q + wide_k), F32),
            ((length, wide_q), BF16),
            ((length, wide_k), BF16),
            ((length, wide_k), BF16),
            ((heads, length, length), F32),
            ((length, wide_q), BF16),
            ((length, width), F32),
            ((length, width), F32),
            ((length, width), BF16),
            ((8, width), F32),
        ],
        4 * length * mine.size,
        [],
        side,
        source,
        *weights,
        gain_q,
        gain_k,
        cosine,
        sine,
        segments[None],
        segments[:, None],
        smem=1,
        room=62,
    )

    def put(half, blocks):
        def made(arrays):
            for n, (_, place) in enumerate(places):
                block = blocks()[n]
                arrays = [
                    lax.dynamic_update_slice_in_dim(w, block[i : i + 1], half * count + place, 0)
                    for i, w in enumerate(arrays)
                ]
            return arrays

        return made

    held = Held(
        [jnp.zeros((links.nf, rows, most), BF16) for _ in range(3)],
        [
            lambda arrays: arrays,
            put(links.mine, lambda: fetch.got),
            put(links.other, lambda: fetch.got[count]),
        ],
    )
    plans = ([(fetch, count - 6, 1)], [(fetch, 1, 0)], [])
    team_in = list(spread(links, normed_two, plans, held))
    early = count - 2
    ffn_w = held.arrays
    ffn_w = [w.reshape(links.nf * rows, most) for w in ffn_w]

    def wave(kernel, blocks, *more):
        size = len(blocks) * length
        kept = [((size, width), BF16)] + [((size, most), BF16)] * (3 if not more else 2)
        out = call(
            functools.partial(kernel, len(blocks)),
            kept + [((length, width), F32 if n == 0 else BF16) for n in blocks],
            1 << 20,
            [],
            *blocks.values(),
            *ffn_w,
            *more,
        )
        return out[: len(kept)], dict(zip(blocks, out[len(kept) :]))

    def share(steps, kernel, extra=((),) * 3):
        kept, part = [], {}
        for blocks, more in zip(steps, extra):
            keep, terms = wave(kernel, blocks, *more)
            kept.append(keep)
            part.update(terms)
        return kept, part

    kept, part = share(team_in, ffn_kernel)
    [(own, *got)] = collect(links, [part], ((), (), ()))
    result, ffn_proj_grad, ffn_out_term = call(
        after_kernel,
        [((length, width), BF16), ((length, width), BF16), ((1, width), F32)],
        1 << 20,
        [],
        own,
        *got,
        middle,
        upstream,
        gains,
    )
    kept_back, part = share(
        spread(links, ffn_proj_grad), ffn_back_kernel, [keep[2:] for keep in kept]
    )
    kinds = [
        [k[0] for k in kept_back],
        [k[0] for k in kept],
        [k[1] for k in kept],
        [k[1] for k in kept_back],
        [k[2] for k in kept_back],
    ]

    made = []

    def grads(sends):
        arrays, values = lax.optimization_barrier(
            ([v for kind in kinds for v in kind], [v for v, _ in sends])
        )
        made.extend(
            call(
                functools.partial(ffn_grad_kernel, len(kept)),
                [((3, width // 2, most), BF16)] * 2,
                1 << 20,
                [],
                side,
                *arrays,
                smem=1,
            )
        )
        mine, other = made
        _, (swapped,) = point(links, [], [(other, None)])

        def block(place):
            both = [lax.dynamic_slice_in_dim(v, place * rows, rows, 1) for v in (mine, swapped)]
            return (both[0].astype(F32) + both[1].astype(F32)).astype(BF16)

        back.sends = [
            (functools.partial(block, place), how) for how, place in places_back
        ]
        back.sends.append((lambda: jnp.stack(back.got[:early]), None))
        return [(v, how) for v, (_, how) in zip(values, sends)]

    back = Stream([])
    [(own, *got)] = collect(links, [part], ((), (), ()), hook=grads)
    (own, *got), _ = point(links, [own] + got, [], (back, 0, 1))

    source_grad, mine, other = call(
        functools.partial(attend_back_kernel, heads),
        [
            ((length, width), BF16),
            ((width // 2, wide_w), BF16),
            ((width // 2, wide_w), BF16),
        ],
        1 << 20,
        [pltpu.VMEM((length, wide_p), BF16)],
        side,
        own,
        *got,
        upstream,
        source,
        middle,
        out,
        gains,
        ffn_out_term,
        *weights,
        normed,
        proj,
        query,
        key,
        value,
        probs,
        mixed,
        gain_q,
        gain_k,
        cosine,
        sine,
        smem=1,
    )
    (mine,), (got,) = point(links, [mine], [(other, None)], (back, 1, 2))
    quarter = head_dim // 4
    col = wide_p + 128 - quarter
    small = mine[:8, col : col + quarter]
    sums = Sum(small, col)
    sums.add(got)

    def owned(t, number):
        at = (((links.hi ^ t) % links.half) * TEAM + links.seat(number)) * rows
        first, second = (lax.dynamic_slice_in_dim(v, at, rows, 0) for v in (mine, got))
        return first.astype(F32) + second.astype(F32)

    parts = [{number: owned(t, number) for number in range(TEAM)} for t in teams]
    plans = ([(back, 1, 1)], [(back, 1, 2)], [(back, 2, 1)])
    done = collect(links, parts, plans, sums)
    done = [sum(v.astype(F32) for v in d) for d in done]
    done = [d.astype(BF16) for d in done]
    done[0] = sums.put(done[0])
    sends = [(d, links.cross(t)) for t, d in zip(teams, done)]
    _, got = point(links, [], sends, (back, 2, 1))
    sums.add(got[0])
    total = sums.put(sum(g.astype(F32) for g in got).astype(BF16))
    (total,), (other,) = point(links, [total], [(total, None)], (back, 1, count))
    shard = total.astype(F32) + other.astype(F32)
    both = jnp.where(links.r == 1, total[:8, col : col + quarter], other[:8, col : col + quarter])
    if links.half > 1:
        both = everywhere(links, small)
    gain_sums = both.astype(F32).reshape(2, head_dim)
    gain_shard = shard[:, wide_p : wide_p + 128]
    point(links, [], [], (back, count + 1, 0))
    other_first = back.got.pop(count)
    _, (other_last,) = point(links, [], [(jnp.stack(back.got[early:]), None)])
    order = [how[0] % TEAM for how, _ in places_back[:TEAM]]
    ffn_grads = None
    for t in teams:
        own = back.got[t * TEAM : (t + 1) * TEAM]
        if links.half == 1:
            others = [other_first, other_last]
        else:
            others = [jnp.concatenate([other_first, other_last])[t * TEAM : (t + 1) * TEAM]]
        if rows % 8:
            others = [some[n] for some in others for n in range(some.shape[0])]
            done = jnp.zeros((3,) + w_gate.shape, F32)
            for k, block, other in zip(order, own, others):
                at, _, _ = ffn_window(links.lo ^ k, w_gate.shape[1])
                block = block.astype(F32) + other.astype(F32)
                block = block + lax.dynamic_slice_in_dim(done, at, most, 2)
                done = lax.dynamic_update_slice_in_dim(done, block, at, 2)
            ffn_grads = done if ffn_grads is None else ffn_grads + done
            continue
        done = call(
            functools.partial(ffn_unpack_kernel, order),
            [(w_gate.shape, F32)] * 3,
            1 << 20,
            [],
            seat,
            *own,
            *others,
            smem=1,
            room=62,
        )
        ffn_grads = done if ffn_grads is None else [a + b for a, b in zip(ffn_grads, done)]
    down_grad, gate_grad, up_grad = ffn_grads
    return (
        result[None],
        source_grad[None],
        shard[:, :wide_q],
        shard[:, wide_q : wide_q + wide_k],
        shard[:, wide_q + wide_k : wide_p],
        jnp.transpose(shard[:, wide_p + 128 :]),
        gate_grad,
        up_grad,
        jnp.transpose(down_grad),
        gain_shard[:, 0],
        gain_shard[:, 1],
        gain_shard[:, 2],
        gain_shard[:, 3],
        gain_sums[0],
        gain_sums[1],
    )


def solution(mesh):
    links = Links(mesh)
    rows = P(("fsdp", "rep"), None, None)
    placed = (
        rows,
        P(("fsdp", "rep"), None),
        P("fsdp", None),
        P("fsdp", None),
        P("fsdp", None),
        P(None, "fsdp"),
        P("fsdp", None),
        P("fsdp", None),
        P(None, "fsdp"),
        P("fsdp"),
        P("fsdp"),
        P("fsdp"),
        P("fsdp"),
        P(),
        P(),
        rows,
    )
    return jax.shard_map(
        lambda *arrays: local(links, *arrays),
        mesh=mesh,
        in_specs=placed,
        out_specs=(rows, rows) + placed[2:13] + (P(), P()),
        check_vma=False,
    )
```

```python
import functools

import jax
import jax.numpy as jnp
from jax import lax
from jax.experimental import pallas as pl
from jax.experimental.pallas import tpu as pltpu
from jax.sharding import PartitionSpec as P

eps = 1e-06


def rms_norm(value, gain):
    return value * lax.rsqrt(jnp.mean(value * value, axis=-1, keepdims=True) + eps) * gain


def positions(segments):
    earlier = (segments[None, :] < segments[:, None]).astype(jnp.int32)
    return jnp.arange(segments.shape[0], dtype=jnp.int32) - jnp.sum(earlier, axis=1)


def rope_tables(where, width):
    half = width // 2
    expo = jnp.arange(half, dtype=jnp.float32) * (2.0 / width)
    freq = jnp.exp(-expo * jnp.log(1000000.0))
    angle = where.astype(jnp.float32)[:, None] * freq[None, :]
    return (jnp.cos(angle), jnp.sin(angle))


def rotate(value, cosine, sine):
    half = value.shape[-1] // 2
    first = value[..., :half]
    second = value[..., half:]
    cosine = cosine[:, None, :]
    sine = sine[:, None, :]
    return jnp.concatenate(
        [first * cosine - second * sine, second * cosine + first * sine], axis=-1
    )


def geglu(gate, upper):
    return jax.nn.gelu(gate, approximate=True) * upper


def across_rows(left, right):
    return lax.dot_general(
        left, right, (((0,), (0,)), ((), ())), preferred_element_type=jnp.float32
    )


def against_cols(left, right):
    return lax.dot_general(
        left, right, (((1,), (1,)), ((), ())), preferred_element_type=jnp.float32
    )


def product(left, right):
    return jnp.dot(left, right, preferred_element_type=jnp.float32)


TEAM = 8
BF16 = jnp.bfloat16
F32 = jnp.float32


class Links:
    def __init__(self, mesh):
        self.nf = mesh.shape["fsdp"]
        self.nr = mesh.shape["rep"]
        assert self.nr == 2 and self.nf % (2 * TEAM) == 0 and self.nf & (self.nf - 1) == 0
        self.teams = self.nf // TEAM
        self.half = self.teams // 2

    def place(self):
        self.f = lax.axis_index("fsdp")
        self.r = lax.axis_index("rep")
        self.lo = self.f % TEAM
        self.hi = self.f // TEAM
        side = self.hi // self.half
        self.mine = side ^ self.r
        self.other = side ^ (1 - self.r)

    def seat(self, number):
        first, second = role(number)
        return self.lo ^ jnp.where(self.r == 0, first, second)

    def go(self, value, how):
        if how is None:
            return lax.ppermute(value, "rep", [(0, 1), (1, 0)])
        pairs = [
            (f * self.nr + r, (f ^ how[r]) * self.nr + r)
            for f in range(self.nf)
            for r in range(self.nr)
            if how[r] is not None
        ]
        return lax.ppermute(value, ("fsdp", "rep"), pairs)

    def both(self, offset):
        return offset, offset

    def cross(self, team):
        return team * TEAM, (self.half + team) * TEAM

    def half_rows(self, value, side, axis=0):
        size = value.shape[axis] // 2
        return lax.dynamic_slice_in_dim(value, side * size, size, axis)

    def blocks(self, order):
        return [
            (
                (t * TEAM + k, (self.half + t) * TEAM + k),
                ((self.hi ^ t) % self.half) * TEAM + (self.lo ^ k),
            )
            for t in range(self.half)
            for k in order
        ]


ROLE_BITS = ((1, 2, 4), (2, 4, 1))


def role(number):
    return tuple(
        sum(bits[i] for i in range(3) if number >> i & 1) for bits in ROLE_BITS
    )


class Stream:
    def __init__(self, sends):
        self.sends = list(sends)
        self.got = []
        self.seen = 0

    def oldest(self, count):
        return self.got[self.seen : self.seen + count]

    def waited(self, values):
        self.got[self.seen : self.seen + len(values)] = values
        self.seen += len(values)

    def next(self, count):
        out, self.sends = self.sends[:count], self.sends[count:]
        return [(value() if callable(value) else value, how) for value, how in out]

    def sent(self, values):
        self.got += values


class Held:
    def __init__(self, arrays, steps):
        self.arrays = arrays
        self.steps = steps

    def before(self, n):
        self.arrays = self.steps[n](self.arrays)
        return self.arrays


def everywhere(links, value):
    value = value.astype(F32)
    value = value + links.go(value, None)
    for bit in range(links.nf.bit_length() - 1):
        value = value + links.go(value, links.both(1 << bit))
    return value


def point(links, waits, sends, *streams):
    olds = [stream.oldest(w) for stream, w, _ in streams]
    waits, olds, values = lax.optimization_barrier((waits, olds, [v for v, _ in sends]))
    for (stream, _, _), old in zip(streams, olds):
        stream.waited(old)
    mores = [stream.next(s) for stream, _, s in streams]
    flat = [v for more in mores for v, _ in more]
    waits, olds, values, flat = lax.optimization_barrier((waits, olds, values, flat))
    for (stream, _, _), old in zip(streams, olds):
        stream.got[stream.seen - len(old) : stream.seen] = old
    got = [links.go(v, how) for v, (_, how) in zip(values, sends)]
    flat = iter(flat)
    for (stream, _, _), more in zip(streams, mores):
        stream.sent([links.go(next(flat), how) for _, how in more])
    return waits, got


def spread(links, value, plans=((), (), ()), held=None):
    by = {n: role(n) for n in (1, 2, 4)}

    def step(n, waits, sends):
        (waits, made), got = point(links, [waits, held.before(n) if held else []], sends, *plans[n])
        if held:
            held.arrays = made
        return waits, got

    _, (one, two, four) = step(0, [], [(value, by[n]) for n in (1, 2, 4)])
    yield {0: value, 1: one, 2: two, 4: four}
    sends = [(one, by[2]), (four, by[1]), (two, by[4])]
    near, (three, five, six) = step(1, [one, two, four], sends)
    far, (seven,) = step(2, [three, five], [(six, by[1])])
    yield {3: far[0], 5: far[1], 6: six}
    yield {7: seven}


class Sum:
    def __init__(self, value, col):
        self.value = value
        self.col = col

    def put(self, block):
        rows, cols = self.value.shape
        row = lax.broadcasted_iota(jnp.int32, block.shape, 0)
        col = lax.broadcasted_iota(jnp.int32, block.shape, 1)
        own = (row < rows) & (col >= self.col) & (col < self.col + cols)
        edges = ((0, block.shape[0] - rows), (self.col, block.shape[1] - self.col - cols))
        return jnp.where(own, jnp.pad(self.value, edges), block)

    def add(self, block):
        rows, cols = self.value.shape
        other = block[:rows, self.col : self.col + cols]
        self.value = (self.value.astype(F32) + other.astype(F32)).astype(BF16)


def collect(links, parts, plans, extra=None, hook=None):
    by = {n: role(n) for n in (1, 2, 4)}

    def add(part, number, block):
        return part[number].astype(F32) + block.astype(F32)

    def carry(blocks):
        return [extra.put(b) if extra and i == 0 else b for i, b in enumerate(blocks)]

    def carried(blocks):
        if extra:
            extra.add(blocks[0])

    sends = carry([p[7].astype(BF16) for p in parts])
    _, got = point(links, [], [(v, by[1]) for v in sends], *plans[0])
    carried(got)
    sixes = carry([add(p, 6, v).astype(BF16) for p, v in zip(parts, got)])
    sends = []
    for part, six in zip(parts, sixes):
        sends += [(six, by[4]), (part[5].astype(BF16), by[1]), (part[3].astype(BF16), by[2])]
    if hook:
        sends = hook(sends)
    _, got = point(links, [], sends, *plans[1])
    carried(got)
    twos = carry([add(p, 2, got[3 * i]).astype(BF16) for i, p in enumerate(parts)])
    sends = []
    for i, (part, two) in enumerate(zip(parts, twos)):
        sends.append((two, by[2]))
        for n, j in ((4, 1), (1, 2)):
            sends.append((add(part, n, got[3 * i + j]).astype(BF16), by[n]))
    _, got = point(links, [], sends, *plans[2])
    carried(got)
    return [(p[0], *got[3 * i : 3 * i + 3]) for i, p in enumerate(parts)]


def ffn_cut(width):
    tiles = width // 128
    most = -(-tiles // TEAM)
    return TEAM - (most * TEAM - tiles), most * 128


def ffn_window(seat, width):
    full, most = ffn_cut(width)
    start = seat * most - jnp.maximum(seat - full, 0) * 128
    at = jnp.minimum(start, width - most)
    size = jnp.where(seat < full, most, most - 128)
    return at, start - at, start - at + size


def ffn_pack_kernel(seat_ref, gate_ref, up_ref, down_ref, *out_refs):
    width = gate_ref.shape[1]
    rows, most = out_refs[0].shape[1:]
    col = lax.broadcasted_iota(jnp.int32, (rows, most), 1)
    for k in range(TEAM):
        at, first, end = ffn_window(seat_ref[0] ^ k, width)
        own = (col >= first) & (col < end)
        for i, ref in enumerate((gate_ref, up_ref, down_ref)):
            block = ref[:, pl.ds(pl.multiple_of(at, 128), most)].astype(F32)
            out_refs[k][i] = jnp.where(own, block, 0.0).astype(BF16)


def ffn_unpack_kernel(order, seat_ref, *refs):
    block_refs, other_refs, out_refs = refs[:TEAM], refs[TEAM:-3], refs[-3:]
    width = out_refs[0].shape[1]
    most = block_refs[0].shape[2]
    others = [ref.at[n] for ref in other_refs for n in range(ref.shape[0])]
    less = most - 128

    def place(k, block, other):
        at, first, end = ffn_window(seat_ref[0] ^ k, width)
        start = pl.multiple_of(at + first, 128)
        for skip, size in ((0, most), (0, less), (128, less)):

            @pl.when((end - first == size) & (first == skip))
            def _(skip=skip, size=size):
                cut = slice(skip, skip + size)
                for i, out_ref in enumerate(out_refs):
                    value = block[i, :, cut].astype(F32) + other[i, :, cut].astype(F32)
                    out_ref[:, pl.ds(start, size)] = value

    for k, block, other in zip(order, block_refs, others):
        place(k, block, other)


def pack_kernel(*refs):
    ins, shard_ref = refs[:-1], refs[-1]
    at = 0
    for ref in ins:
        width = ref.shape[1]
        shard_ref[:, at : at + width] = ref[...]
        at += width


def norm_back(value, gain, grad):
    inv = lax.rsqrt(jnp.mean(value * value, axis=-1, keepdims=True) + eps)
    scaled = grad * gain
    mean = jnp.mean(scaled * value, axis=-1, keepdims=True)
    back = scaled * inv - value * (inv * inv * inv * mean)
    return back, jnp.sum(grad * (value * inv), axis=0, keepdims=True)


def turn(value, cosine, sine):
    half = value.shape[-1] // 2
    first, second = value[:, :half], value[:, half:]
    return jnp.concatenate([first * cosine - second * sine, second * cosine + first * sine], 1)


def halves(side, value):
    if isinstance(value, tuple):
        mine, other = value
        first = jnp.where(side == 0, mine, other)
        return jnp.concatenate([first, jnp.where(side == 0, other, mine)], 1)
    half = value.shape[1] // 2
    first, second = value[:, :half], value[:, half:]
    return jnp.where(side == 0, first, second), jnp.where(side == 0, second, first)


def attend_kernel(
    heads,
    side_ref,
    x_ref,
    wm_ref,
    wo_ref,
    gq_ref,
    gk_ref,
    cos_ref,
    sin_ref,
    seg_row_ref,
    seg_col_ref,
    h1_ref,
    proj_ref,
    q_ref,
    k_ref,
    v_ref,
    p_ref,
    a_ref,
    o_ref,
    x2_ref,
    h2_ref,
    gains_ref,
):
    dim = k_ref.shape[1]
    wide_q = heads * dim
    wide_p = wide_q + 2 * dim
    length = x_ref.shape[0]
    source = x_ref[...].astype(F32)
    side = side_ref[0]
    gains = [jnp.transpose(w[:, wide_p : wide_p + 128].astype(F32))[:8] for w in (wm_ref, wo_ref)]
    gains = halves(side, tuple(gains))
    gains_ref[...] = gains
    h1 = rms_norm(source, gains[0:1])
    h1_ref[...] = h1.astype(BF16)
    h1m, h1o = halves(side, h1)
    proj = product(h1m.astype(BF16), wm_ref[:, :wide_p])
    proj = proj + product(h1o.astype(BF16), wo_ref[:, :wide_p])
    proj_ref[...] = proj[:, : wide_q + dim]
    value = proj[:, wide_q + dim :].astype(BF16)
    v_ref[...] = value
    cosine, sine = cos_ref[...], sin_ref[...]
    key = turn(rms_norm(proj[:, wide_q : wide_q + dim], gk_ref[...]), cosine, sine).astype(BF16)
    k_ref[...] = key
    row = lax.broadcasted_iota(jnp.int32, (length, length), 0)
    col = lax.broadcasted_iota(jnp.int32, (length, length), 1)
    allowed = (seg_col_ref[...] == seg_row_ref[...]) & (col <= row)
    for h in range(heads):
        cut = slice(h * dim, (h + 1) * dim)
        query = turn(rms_norm(proj[:, cut], gq_ref[...]), cosine, sine).astype(BF16)
        q_ref[:, cut] = query
        logits = jnp.where(allowed, against_cols(query, key) * dim ** (-0.5), -1e30)
        expo = jnp.exp(logits - jnp.max(logits, axis=-1, keepdims=True))
        probs = expo / jnp.sum(expo, axis=-1, keepdims=True)
        p_ref[h] = probs
        a_ref[:, cut] = product(probs.astype(BF16), value).astype(BF16)
    mixed = a_ref[...]
    out = [against_cols(mixed, w[:, wide_p + 128 :]) for w in (wm_ref, wo_ref)]
    out = halves(side, tuple(out))
    o_ref[...] = out
    middle = source + rms_norm(out, gains[1:2])
    x2_ref[...] = middle
    h2_ref[...] = rms_norm(middle, gains[2:3]).astype(BF16)


def added(own_ref, refs):
    value = own_ref[...]
    for ref in refs:
        value = value + ref[...].astype(F32)
    return value


def after_kernel(own_ref, *refs):
    x2_ref, c_ref, gains_ref, result_ref, df_ref, term_ref = refs[3:]
    value = added(own_ref, refs[:3])
    gain = gains_ref[3:4]
    result_ref[...] = (x2_ref[...] + rms_norm(value, gain)).astype(BF16)
    back, term = norm_back(value, gain, c_ref[...].astype(F32))
    df_ref[...] = back.astype(BF16)
    term_ref[...] = term


def attend_back_kernel(
    heads,
    side_ref,
    own_ref,
    *refs,
):
    got_refs, refs = refs[:3], refs[3:]
    (
    c_ref,
    x_ref,
    x2_ref,
    o_ref,
    gains_ref,
    ffn_out_ref,
    wm_ref,
    wo_ref,
    h1_ref,
    proj_ref,
    q_ref,
    k_ref,
    v_ref,
    p_ref,
    a_ref,
    gq_ref,
    gk_ref,
    cos_ref,
    sin_ref,
    grad_ref,
    mine_ref,
    other_ref,
    low_ref,
    ) = refs
    dim = k_ref.shape[1]
    wide_q = heads * dim
    wide_p = wide_q + 2 * dim
    side = side_ref[0]
    scale = dim ** (-0.5)
    gains = gains_ref[...]
    back, ffn_in_term = norm_back(x2_ref[...], gains[2:3], added(own_ref, got_refs))
    middle = c_ref[...].astype(F32) + back
    out_back, attn_out_term = norm_back(o_ref[...], gains[1:2], middle)
    out_low = [v.astype(BF16) for v in halves(side, out_back)]
    mixed = product(out_low[0], wm_ref[:, wide_p + 128 :])
    mixed = (mixed + product(out_low[1], wo_ref[:, wide_p + 128 :])).astype(BF16)
    key, value = k_ref[...], v_ref[...]
    cosine, sine = cos_ref[...], sin_ref[...]
    key_back, value_back, query_gain = 0.0, 0.0, 0.0
    for h in range(heads):
        cut = slice(h * dim, (h + 1) * dim)
        probs = p_ref[h]
        mixed_h = mixed[:, cut]
        probs_back = against_cols(mixed_h, value)
        value_back = value_back + across_rows(probs.astype(BF16), mixed_h)
        row_dot = jnp.sum(probs * probs_back, axis=-1, keepdims=True)
        score = (probs * (probs_back - row_dot) * scale).astype(BF16)
        key_back = key_back + across_rows(score, q_ref[:, cut])
        query_back = product(score, key).astype(BF16).astype(F32)
        query_back, term = norm_back(
            proj_ref[:, cut], gq_ref[...], turn(query_back, cosine, -sine)
        )
        query_gain = query_gain + term
        low_ref[:, cut] = query_back.astype(BF16)
    key_back = key_back.astype(BF16).astype(F32)
    key_back, key_gain = norm_back(
        proj_ref[:, wide_q : wide_q + dim], gk_ref[...], turn(key_back, cosine, -sine)
    )
    low_ref[:, wide_q : wide_q + dim] = key_back.astype(BF16)
    low_ref[:, wide_q + dim :] = value_back.astype(BF16)
    quarter = dim // 4
    small = [
        gain[:, i * quarter : (i + 1) * quarter]
        for gain in (query_gain, key_gain)
        for i in range(4)
    ]
    small = jnp.concatenate(small, 0)
    small = jnp.concatenate([jnp.zeros((8, 128 - quarter), F32), small], 1)
    low = low_ref[...]
    source = x_ref[...].astype(F32)
    back = [against_cols(low, w[:, :wide_p]) for w in (wm_ref, wo_ref)]
    back, attn_in_term = norm_back(source, gains[0:1], halves(side, tuple(back)))
    grad_ref[...] = (middle + back).astype(BF16)
    terms = jnp.concatenate([attn_in_term, attn_out_term, ffn_in_term, ffn_out_ref[...]], 0)
    terms = jnp.concatenate([terms, jnp.zeros((124, terms.shape[1]), F32)], 0)
    terms = halves(side, terms)
    h1 = halves(side, h1_ref[...].astype(F32))
    mixed_low = a_ref[...]
    for i, ref in enumerate((mine_ref, other_ref)):
        block = jnp.transpose(terms[i])
        ref[:, wide_p : wide_p + 128] = jnp.concatenate([block[:8] + small, block[8:]], 0).astype(BF16)
        ref[:, :wide_p] = across_rows(h1[i].astype(BF16), low).astype(BF16)
        ref[:, wide_p + 128 :] = across_rows(out_low[i], mixed_low).astype(BF16)


def chunks(width):
    return [slice(at, min(at + 256, width)) for at in range(0, width, 256)]


def ffn_kernel(count, *refs):
    block_refs, refs = refs[:count], refs[count:]
    gate_ref, up_ref, down_ref, x_ref, hid_ref, by_gate_ref, by_up_ref, *out_refs = refs
    rows = block_refs[0].shape[0]
    x = jnp.concatenate([ref[...] for ref in block_refs], 0)
    x_ref[...] = x
    root = (2.0 / 3.141592653589793) ** 0.5
    for cut in chunks(gate_ref.shape[1]):
        gate = product(x, gate_ref[:, cut])
        upper = product(x, up_ref[:, cut])
        square = gate * gate
        bent = jnp.tanh(root * gate * (1.0 + 0.044715 * square))
        half = 0.5 * (1.0 + bent)
        gelu = gate * half
        slope = half + 0.5 * gate * (1.0 - bent * bent) * root * (1.0 + 3 * 0.044715 * square)
        hid_ref[:, cut] = (gelu * upper).astype(BF16)
        by_gate_ref[:, cut] = (upper * slope).astype(BF16)
        by_up_ref[:, cut] = gelu.astype(BF16)
    out = against_cols(hid_ref[...], down_ref[...])
    for i, ref in enumerate(out_refs):
        ref[...] = out[i * rows : (i + 1) * rows].astype(ref.dtype)


def ffn_back_kernel(count, *refs):
    block_refs, refs = refs[:count], refs[count:]
    gate_ref, up_ref, down_ref, by_gate_ref, by_up_ref, df_ref, dgt_ref, dup_ref, *out_refs = refs
    rows = block_refs[0].shape[0]
    df = jnp.concatenate([ref[...] for ref in block_refs], 0)
    df_ref[...] = df
    for cut in chunks(gate_ref.shape[1]):
        grad = product(df, down_ref[:, cut])
        dgt_ref[:, cut] = (grad * by_gate_ref[:, cut].astype(F32)).astype(BF16)
        dup_ref[:, cut] = (grad * by_up_ref[:, cut].astype(F32)).astype(BF16)
    out = against_cols(dgt_ref[...], gate_ref[...]) + against_cols(dup_ref[...], up_ref[...])
    for i, ref in enumerate(out_refs):
        ref[...] = out[i * rows : (i + 1) * rows].astype(ref.dtype)


def ffn_grad_kernel(count, side_ref, *refs):
    def whole(kind):
        return jnp.concatenate([ref[...] for ref in refs[kind * count : (kind + 1) * count]], 0)

    mine_ref, other_ref = refs[5 * count :]
    side = side_ref[0]
    left = [[v.astype(BF16) for v in halves(side, whole(i).astype(F32))] for i in (0, 1)]
    for i, (pair, right) in enumerate(((0, 2), (1, 3), (1, 4))):
        right = whole(right)
        for half, ref in zip(left[pair], (mine_ref, other_ref)):
            ref[i] = across_rows(half, right).astype(BF16)


def call(kernel, outs, flops, scratch, *arrays, smem=0, room=32):
    size = 1 << 16
    spaces = [pltpu.SMEM] * smem + [None] * (len(arrays) - smem)
    return pl.pallas_call(
        kernel,
        out_shape=[jax.ShapeDtypeStruct(shape, kind) for shape, kind in outs],
        in_specs=[pl.BlockSpec(memory_space=space) for space in spaces],
        scratch_shapes=scratch,
        cost_estimate=pl.CostEstimate(flops=flops, bytes_accessed=size, transcendentals=0),
        compiler_params=pltpu.CompilerParams(vmem_limit_bytes=room << 20),
    )(*arrays)


def local(
    links,
    tokens,
    segment_ids,
    w_query,
    w_key,
    w_value,
    w_out,
    w_gate,
    w_up,
    w_down,
    g_attn_in,
    g_attn_out,
    g_ffn_in,
    g_ffn_out,
    g_query,
    g_key,
    cotangent,
):
    links.place()
    rows = w_query.shape[0]
    segments = segment_ids[0]
    head_dim = g_query.shape[0]
    wide_q = w_query.shape[1]
    wide_k = w_key.shape[1]
    wide_p = wide_q + 2 * wide_k
    wide_w = wide_p + 128 + wide_q
    heads = wide_q // head_dim
    length, width = tokens.shape[1:]
    most = ffn_cut(w_gate.shape[1])[1]
    seat = links.lo[None].astype(jnp.int32)
    source, upstream = tokens[0], cotangent[0]

    gains = jnp.pad(jnp.stack([g_attn_in, g_attn_out, g_ffn_in, g_ffn_out], 1), ((0, 0), (0, 124)))
    (shard,) = call(
        pack_kernel,
        [((rows, wide_w), BF16)],
        1 << 20,
        [],
        w_query,
        w_key,
        w_value,
        gains,
        jnp.transpose(w_out),
        room=62,
    )
    packed = call(
        ffn_pack_kernel,
        [((3, rows, most), BF16)] * TEAM,
        1 << 20,
        [],
        seat,
        w_gate,
        w_up,
        jnp.transpose(w_down),
        smem=1,
        room=62,
    )
    places = links.blocks((0, 3, 4, 7, 1, 2, 5, 6))
    places_back = links.blocks((6, 7, 4, 5, 0, 1, 2, 3))
    count = len(places)
    fetch = Stream((packed[how[0] % TEAM], how) for how, _ in places)
    teams = range(links.half)
    _, crossed = point(links, [], [(shard, links.cross(t)) for t in teams])
    fetch.sends.append((lambda: jnp.stack(fetch.got[:count]), None))
    got = {}
    for some in spread(
        links,
        jnp.stack(crossed) if links.half > 1 else crossed[0][None],
        ([(fetch, 0, 2)], [(fetch, 2, 2)], [(fetch, 2, 2)]),
    ):
        got.update(some)
    mine = jnp.zeros((count, rows, wide_w), BF16)
    for number in range(TEAM):
        for t in teams:
            at = ((links.hi ^ t) % links.half) * TEAM + links.seat(number)
            mine = lax.dynamic_update_slice_in_dim(mine, got[number][t : t + 1], at, 0)
    mine = mine.reshape(count * rows, wide_w)
    (mine,), (other,) = point(links, [mine], [(mine, None)], (fetch, 2, count - 6))
    weights = (mine, other)
    side = links.mine[None].astype(jnp.int32)

    cosine, sine = rope_tables(positions(segments), head_dim)
    gain_q = g_query.astype(F32)[None]
    gain_k = g_key.astype(F32)[None]
    normed, proj, query, key, value, probs, mixed, out, middle, normed_two, gains = call(
        functools.partial(attend_kernel, heads),
        [
            ((length, width), BF16),
            ((length, wide_q + wide_k), F32),
            ((length, wide_q), BF16),
            ((length, wide_k), BF16),
            ((length, wide_k), BF16),
            ((heads, length, length), F32),
            ((length, wide_q), BF16),
            ((length, width), F32),
            ((length, width), F32),
            ((length, width), BF16),
            ((8, width), F32),
        ],
        4 * length * mine.size,
        [],
        side,
        source,
        *weights,
        gain_q,
        gain_k,
        cosine,
        sine,
        segments[None],
        segments[:, None],
        smem=1,
        room=62,
    )

    def put(half, blocks):
        def made(arrays):
            for n, (_, place) in enumerate(places):
                block = blocks()[n]
                arrays = [
                    lax.dynamic_update_slice_in_dim(w, block[i : i + 1], half * count + place, 0)
                    for i, w in enumerate(arrays)
                ]
            return arrays

        return made

    held = Held(
        [jnp.zeros((links.nf, rows, most), BF16) for _ in range(3)],
        [
            lambda arrays: arrays,
            put(links.mine, lambda: fetch.got),
            put(links.other, lambda: fetch.got[count]),
        ],
    )
    plans = ([(fetch, count - 6, 1)], [(fetch, 1, 0)], [])
    team_in = list(spread(links, normed_two, plans, held))
    early = count - 2
    ffn_w = held.arrays
    ffn_w = [w.reshape(links.nf * rows, most) for w in ffn_w]

    def wave(kernel, blocks, *more):
        size = len(blocks) * length
        kept = [((size, width), BF16)] + [((size, most), BF16)] * (3 if not more else 2)
        out = call(
            functools.partial(kernel, len(blocks)),
            kept + [((length, width), F32 if n == 0 else BF16) for n in blocks],
            1 << 20,
            [],
            *blocks.values(),
            *ffn_w,
            *more,
        )
        return out[: len(kept)], dict(zip(blocks, out[len(kept) :]))

    def share(steps, kernel, extra=((),) * 3):
        kept, part = [], {}
        for blocks, more in zip(steps, extra):
            keep, terms = wave(kernel, blocks, *more)
            kept.append(keep)
            part.update(terms)
        return kept, part

    kept, part = share(team_in, ffn_kernel)
    [(own, *got)] = collect(links, [part], ((), (), ()))
    result, ffn_proj_grad, ffn_out_term = call(
        after_kernel,
        [((length, width), BF16), ((length, width), BF16), ((1, width), F32)],
        1 << 20,
        [],
        own,
        *got,
        middle,
        upstream,
        gains,
    )
    kept_back, part = share(
        spread(links, ffn_proj_grad), ffn_back_kernel, [keep[2:] for keep in kept]
    )
    kinds = [
        [k[0] for k in kept_back],
        [k[0] for k in kept],
        [k[1] for k in kept],
        [k[1] for k in kept_back],
        [k[2] for k in kept_back],
    ]

    made = []

    def grads(sends):
        arrays, values = lax.optimization_barrier(
            ([v for kind in kinds for v in kind], [v for v, _ in sends])
        )
        made.extend(
            call(
                functools.partial(ffn_grad_kernel, len(kept)),
                [((3, width // 2, most), BF16)] * 2,
                1 << 20,
                [],
                side,
                *arrays,
                smem=1,
            )
        )
        mine, other = made
        _, (swapped,) = point(links, [], [(other, None)])

        def block(place):
            both = [lax.dynamic_slice_in_dim(v, place * rows, rows, 1) for v in (mine, swapped)]
            return (both[0].astype(F32) + both[1].astype(F32)).astype(BF16)

        back.sends = [
            (functools.partial(block, place), how) for how, place in places_back
        ]
        back.sends.append((lambda: jnp.stack(back.got[:early]), None))
        return [(v, how) for v, (_, how) in zip(values, sends)]

    back = Stream([])
    [(own, *got)] = collect(links, [part], ((), (), ()), hook=grads)
    (own, *got), _ = point(links, [own] + got, [], (back, 0, 1))

    source_grad, mine, other = call(
        functools.partial(attend_back_kernel, heads),
        [
            ((length, width), BF16),
            ((width // 2, wide_w), BF16),
            ((width // 2, wide_w), BF16),
        ],
        1 << 20,
        [pltpu.VMEM((length, wide_p), BF16)],
        side,
        own,
        *got,
        upstream,
        source,
        middle,
        out,
        gains,
        ffn_out_term,
        *weights,
        normed,
        proj,
        query,
        key,
        value,
        probs,
        mixed,
        gain_q,
        gain_k,
        cosine,
        sine,
        smem=1,
    )
    (mine,), (got,) = point(links, [mine], [(other, None)], (back, 1, 2))
    quarter = head_dim // 4
    col = wide_p + 128 - quarter
    small = mine[:8, col : col + quarter]
    sums = Sum(small, col)
    sums.add(got)

    def owned(t, number):
        at = (((links.hi ^ t) % links.half) * TEAM + links.seat(number)) * rows
        first, second = (lax.dynamic_slice_in_dim(v, at, rows, 0) for v in (mine, got))
        return first.astype(F32) + second.astype(F32)

    parts = [{number: owned(t, number) for number in range(TEAM)} for t in teams]
    plans = ([(back, 1, 1)], [(back, 1, 2)], [(back, 2, 1)])
    done = collect(links, parts, plans, sums)
    done = [sum(v.astype(F32) for v in d) for d in done]
    done = [d.astype(BF16) for d in done]
    done[0] = sums.put(done[0])
    sends = [(d, links.cross(t)) for t, d in zip(teams, done)]
    _, got = point(links, [], sends, (back, 2, 1))
    sums.add(got[0])
    total = sums.put(sum(g.astype(F32) for g in got).astype(BF16))
    (total,), (other,) = point(links, [total], [(total, None)], (back, 1, count))
    shard = total.astype(F32) + other.astype(F32)
    both = jnp.where(links.r == 1, total[:8, col : col + quarter], other[:8, col : col + quarter])
    if links.half > 1:
        both = everywhere(links, small)
    gain_sums = both.astype(F32).reshape(2, head_dim)
    gain_shard = shard[:, wide_p : wide_p + 128]
    point(links, [], [], (back, count + 1, 0))
    other_first = back.got.pop(count)
    _, (other_last,) = point(links, [], [(jnp.stack(back.got[early:]), None)])
    order = [how[0] % TEAM for how, _ in places_back[:TEAM]]
    ffn_grads = None
    for t in teams:
        own = back.got[t * TEAM : (t + 1) * TEAM]
        if links.half == 1:
            others = [other_first, other_last]
        else:
            others = [jnp.concatenate([other_first, other_last])[t * TEAM : (t + 1) * TEAM]]
        if rows % 8:
            others = [some[n] for some in others for n in range(some.shape[0])]
            done = jnp.zeros((3,) + w_gate.shape, F32)
            for k, block, other in zip(order, own, others):
                at, _, _ = ffn_window(links.lo ^ k, w_gate.shape[1])
                block = block.astype(F32) + other.astype(F32)
                block = block + lax.dynamic_slice_in_dim(done, at, most, 2)
                done = lax.dynamic_update_slice_in_dim(done, block, at, 2)
            ffn_grads = done if ffn_grads is None else ffn_grads + done
            continue
        done = call(
            functools.partial(ffn_unpack_kernel, order),
            [(w_gate.shape, F32)] * 3,
            1 << 20,
            [],
            seat,
            *own,
            *others,
            smem=1,
            room=62,
        )
        ffn_grads = done if ffn_grads is None else [a + b for a, b in zip(ffn_grads, done)]
    down_grad, gate_grad, up_grad = ffn_grads
    return (
        result[None],
        source_grad[None],
        shard[:, :wide_q],
        shard[:, wide_q : wide_q + wide_k],
        shard[:, wide_q + wide_k : wide_p],
        jnp.transpose(shard[:, wide_p + 128 :]),
        gate_grad,
        up_grad,
        jnp.transpose(down_grad),
        gain_shard[:, 0],
        gain_shard[:, 1],
        gain_shard[:, 2],
        gain_shard[:, 3],
        gain_sums[0],
        gain_sums[1],
    )


def solution(mesh):
    links = Links(mesh)
    rows = P(("fsdp", "rep"), None, None)
    placed = (
        rows,
        P(("fsdp", "rep"), None),
        P("fsdp", None),
        P("fsdp", None),
        P("fsdp", None),
        P(None, "fsdp"),
        P("fsdp", None),
        P("fsdp", None),
        P(None, "fsdp"),
        P("fsdp"),
        P("fsdp"),
        P("fsdp"),
        P("fsdp"),
        P(),
        P(),
        rows,
    )
    return jax.shard_map(
        lambda *arrays: local(links, *arrays),
        mesh=mesh,
        in_specs=placed,
        out_specs=(rows, rows) + placed[2:13] + (P(), P()),
        check_vma=False,
    )
```
